512 devices in a mesh: seq: 64 (over y_hi, z, core), tp: 8 (over y_lo, x).
Axes of the slice: x: 4, y: 4 (y_hi: 2, y_lo: 2; y = y_hi * 2 + y_lo), z: 16, core: 2. Of those that a mesh axis runs over, the one named last changes fastest.
Arguments:
- queries: bfloat16 [32768, 4096], P('seq', 'tp'), may hold values from -3 to 3
- keys: bfloat16 [32768, 4096], P('seq', 'tp'), may hold values from -3 to 3
- values: bfloat16 [32768, 4096], P('seq', 'tp'), may hold values from -6 to 6
- out_grad: bfloat16 [32768, 4096], P('seq', 'tp'), may hold values from -6 to 6
- gain: float32 [4096], P('tp'), may hold values from 0.5 to 1.5
- log_decay: float32 [32768, 32], P('seq', 'tp'), may hold values from -1 to 0, as said below
Outputs:
- query_grad: bfloat16 [32768, 4096], P('seq', 'tp')
- key_grad: bfloat16 [32768, 4096], P('seq', 'tp')
- value_grad: bfloat16 [32768, 4096], P('seq', 'tp')
- gain_grad: float32 [4096], P(('tp', 'seq'))
The draws below stay inside these ranges and needn't reach their ends.
Inputs may be any that keep to these rules, and one draw needn't show every extreme that they name: `log_decay`: every entry is negative.
All inputs are finite; a program needn't handle non-finite values.
Results may differ from the reference program's by a relative error of at most 0.02.
Values may be sent and summed in bfloat16 or wider, within the bound.
No kernel may reach another device: no remote copies, remote signals or barrier semaphores. Data moves between devices by JAX's collectives and lax.ppermute only.
A program may use at most 64 MiB of HBM per device.

```python
import math
import jax
import jax.numpy as jnp
from jax import lax

HEAD_GROUP = 32
HD = 128
TOK_DEV = 512
TOKEN_COUNT = 32768


def draw_log_decay(key, part):
    key = jax.random.fold_in(key, 11)
    key_sequence = jax.random.split(key, 8)
    fast_count = HEAD_GROUP // 2
    order = jax.random.permutation(key_sequence[0], HEAD_GROUP)
    is_fast = order < fast_count
    slow_rate = jnp.exp(jax.random.uniform(key_sequence[1], (HEAD_GROUP,), minval=math.log(0.1), maxval=math.log(0.8))) / TOKEN_COUNT
    fast_rate = jnp.exp(jax.random.uniform(key_sequence[2], (HEAD_GROUP,), minval=math.log(1.0 / 50.0), maxval=math.log(1.0 / 30.0)))
    head_decay_rate = jnp.where(is_fast, fast_rate, slow_rate)
    block_count = TOKEN_COUNT // TOK_DEV
    slow_factor = jnp.exp(jax.random.uniform(key_sequence[3], (block_count, HEAD_GROUP), minval=-0.7, maxval=0.7))
    fast_factor = jnp.exp(jax.random.uniform(key_sequence[7], (block_count, HEAD_GROUP), minval=-6.0, maxval=0.7))
    block_factor = jnp.repeat(jnp.where(is_fast[None], fast_factor, slow_factor), TOK_DEV, axis=0)
    jaggedness = jax.random.uniform(key_sequence[4], (TOKEN_COUNT, HEAD_GROUP), minval=0.5, maxval=1.5)
    segments = jax.random.uniform(key_sequence[5], (TOKEN_COUNT, HEAD_GROUP)) < 2.0 / TOKEN_COUNT
    segment_depth = jax.random.uniform(key_sequence[6], (TOKEN_COUNT, HEAD_GROUP), minval=math.log(0.5), maxval=math.log(0.8))
    return (-head_decay_rate[None] * block_factor * jaggedness + jnp.where(segments, segment_depth, 0.0)).astype(jnp.float32)


def steps_of(own_key, dims, shards, smallest, largest):
    level = 1.0
    for position, shards_of in shards:
        steps = jax.random.uniform(jax.random.fold_in(jax.random.fold_in(own_key, 6), position), (shards_of,), jnp.float32, smallest / len(shards), largest / len(shards))
        level = level * jnp.repeat(jnp.exp(steps), dims[position] // shards_of).reshape((-1,) + (1,) * (len(dims) - 1 - position))
    return level


def centred(own_key, dims, scale, bound, cuts=(), held_as=jnp.bfloat16):
    result = scale * jax.random.normal(own_key, dims, jnp.float32)
    if cuts:
        result = result * steps_of(own_key, dims, cuts, -0.22, 0.18)
    return jnp.clip(result, -bound, bound).astype(held_as)


def setup_inputs(seed: int = 0) -> dict:
    splits = jax.random.split(jax.random.key(seed), 7)
    queries = centred(splits[0], (TOKEN_COUNT, HEAD_GROUP * HD), 0.3, 3.0, ((0, 64), (1, 8)))
    keys = centred(splits[1], (TOKEN_COUNT, HEAD_GROUP * HD), 0.3, 3.0, ((0, 64), (1, 8)))
    values = centred(splits[2], (TOKEN_COUNT, HEAD_GROUP * HD), 1.0, 6.0, ((0, 64), (1, 8)))
    out_grad = centred(splits[3], (TOKEN_COUNT, HEAD_GROUP * HD), 1.0, 6.0, ((0, 64), (1, 8)))
    gain = jnp.clip(1.0 + 0.1 * jax.random.normal(splits[4], (HEAD_GROUP * HD,), jnp.float32), 0.5, 1.5)
    log_decay = draw_log_decay(jax.random.fold_in(splits[6], 71), 0)
    return {"queries": queries, "keys": keys, "values": values, "out_grad": out_grad, "gain": gain, "log_decay": log_decay}


def decay_table(cumulative):
    length = cumulative.shape[0]
    row_index = jnp.arange(length)[:, None]
    col_index = jnp.arange(length)[None, :]
    causal = (row_index >= col_index)[None]
    spread_logs = cumulative.T[:, :, None] - cumulative.T[:, None, :]
    return jnp.where(causal, jnp.exp(jnp.where(causal, spread_logs, 0.0)), 0.0)

def reference(queries, keys, values, out_grad, gain, log_decay):
    block_count = TOKEN_COUNT // TOK_DEV
    shaped = (block_count, TOK_DEV, HEAD_GROUP, HD)
    query_blocks = queries.reshape(shaped)
    key_blocks = keys.reshape(shaped)
    value_blocks = values.reshape(shaped)
    decay_blocks = log_decay.reshape(block_count, TOK_DEV, HEAD_GROUP)

    def forward_step(carried_state, inputs):
        query_rows, key_rows, value_rows, logs = inputs
        cumulative = jnp.cumsum(logs, axis=0)
        block_total = cumulative[-1]
        weights = decay_table(cumulative)
        scores = jnp.einsum('thd,shd->hts', query_rows.astype(jnp.float32), key_rows.astype(jnp.float32))
        score_weights = (weights * scores).astype(jnp.bfloat16)
        state_half = carried_state.astype(jnp.bfloat16)
        inner_part = jnp.einsum('hts,she->the', score_weights.astype(jnp.float32), value_rows.astype(jnp.float32))
        carried = jnp.exp(cumulative)[:, :, None] * jnp.einsum('thd,hde->the', query_rows.astype(jnp.float32), state_half.astype(jnp.float32))
        scaled_keys = (key_rows.astype(jnp.float32) * jnp.exp(block_total[None] - cumulative)[:, :, None]).astype(jnp.bfloat16)
        update = jnp.einsum('thd,the->hde', scaled_keys.astype(jnp.float32), value_rows.astype(jnp.float32)).astype(jnp.bfloat16)
        new_state = jnp.exp(block_total)[:, None, None] * carried_state + update.astype(jnp.float32)
        return (new_state, (inner_part + carried, state_half))
    empty_state = jnp.zeros((HEAD_GROUP, HD, HD), jnp.float32)
    unused, (outputs, halves) = lax.scan(forward_step, empty_state, (query_blocks, key_blocks, value_blocks, decay_blocks))
    attention = outputs.reshape(TOKEN_COUNT, HEAD_GROUP * HD)
    feature_count = HEAD_GROUP * HD
    upstream = gain[None] * out_grad.astype(jnp.float32)
    mean_square = lax.optimization_barrier(jnp.sum(attention * attention, axis=1)) / feature_count
    mean_dot = lax.optimization_barrier(jnp.sum(attention * upstream, axis=1)) / feature_count
    inverse = lax.rsqrt(mean_square + 1e-05)
    attn_grad = (inverse[:, None] * upstream - (inverse * inverse * inverse * mean_dot)[:, None] * attention).astype(jnp.bfloat16)
    gain_grad = lax.optimization_barrier(jnp.sum(out_grad.astype(jnp.float32) * attention * inverse[:, None], axis=0))
    grad_blocks = attn_grad.reshape(shaped)

    def backward_step(carried_state, inputs):
        query_rows, key_rows, value_rows, logs, grad_rows, state_half = inputs
        cumulative = jnp.cumsum(logs, axis=0)
        block_total = cumulative[-1]
        weights = decay_table(cumulative)
        query_wide = query_rows.astype(jnp.float32)
        key_wide = key_rows.astype(jnp.float32)
        value_wide = value_rows.astype(jnp.float32)
        grad_wide = grad_rows.astype(jnp.float32)
        scores = jnp.einsum('thd,shd->hts', query_wide, key_wide)
        score_weights = (weights * scores).astype(jnp.bfloat16).astype(jnp.float32)
        grad_scores = jnp.einsum('the,she->hts', grad_wide, value_wide)
        grad_mix = (weights * grad_scores).astype(jnp.bfloat16).astype(jnp.float32)
        back_half = carried_state.astype(jnp.bfloat16).astype(jnp.float32)
        exp_cum = jnp.exp(cumulative)[:, :, None]
        exp_rest = jnp.exp(block_total[None] - cumulative)[:, :, None]
        query_grad = jnp.einsum('hts,shd->thd', grad_mix, key_wide) + exp_cum * jnp.einsum('the,hde->thd', grad_wide, state_half.astype(jnp.float32))
        key_grad = jnp.einsum('hts,thd->shd', grad_mix, query_wide) + exp_rest * jnp.einsum('hde,the->thd', back_half, value_wide)
        value_grad = jnp.einsum('hts,the->she', score_weights, grad_wide) + exp_rest * jnp.einsum('hde,thd->the', back_half, key_wide)
        scaled_queries = (query_wide * exp_cum).astype(jnp.bfloat16)
        back_update = jnp.einsum('thd,the->hde', scaled_queries.astype(jnp.float32), grad_wide).astype(jnp.bfloat16)
        new_state = jnp.exp(block_total)[:, None, None] * carried_state + back_update.astype(jnp.float32)
        return (new_state, (query_grad.astype(jnp.bfloat16), key_grad.astype(jnp.bfloat16), value_grad.astype(jnp.bfloat16)))
    unused, (query_grads, key_grads, value_grads) = lax.scan(backward_step, empty_state, (query_blocks, key_blocks, value_blocks, decay_blocks, grad_blocks, halves), reverse=True)
    flat = (TOKEN_COUNT, HEAD_GROUP * HD)
    return (query_grads.reshape(flat), key_grads.reshape(flat), value_grads.reshape(flat), gain_grad)
```

```python
import jax
import jax.numpy as jnp
from jax import lax
from jax.experimental import pallas as pl
from jax.experimental.pallas import tpu as pltpu
from jax.sharding import PartitionSpec as P

HEAD_GROUP = 32
HD = 128
SIDE = 8
PIECE = 64
MESSAGE = PIECE + 16
TILE = 128
BF16, F32 = jnp.bfloat16, jnp.float32

NEAR = [[g * SIDE + m for m in range(SIDE)] for g in range(SIDE)]
FAR = [[g * SIDE + m for g in range(SIDE)] for m in range(SIDE)]


def mm(a, b):
    return lax.dot_general(a, b, (((1,), (0,)), ((), ())), preferred_element_type=F32)


def mm_nt(a, b):
    return lax.dot_general(a, b, (((1,), (1,)), ((), ())), preferred_element_type=F32)


def mm_tn(a, b):
    return lax.dot_general(a, b, (((0,), (0,)), ((), ())), preferred_element_type=F32)


def split3(x):
    high = x.astype(BF16)
    rest = x - high.astype(F32)
    mid = rest.astype(BF16)
    low = (rest - mid.astype(F32)).astype(BF16)
    return high, mid, low


def head(ref, h):
    return ref[:, h * HD : (h + 1) * HD]


def iota(shape, dim):
    return lax.broadcasted_iota(jnp.int32, shape, dim)


def scalar_rows(total):
    high, mid, low = (part.astype(F32) for part in split3(total))
    rows = iota((16, HD), 0)
    out = jnp.where(rows == 0, high, jnp.where(rows == 1, mid, jnp.where(rows == 2, low, 0.0)))
    return out.astype(BF16)


def read_scalar_row(tile):
    wide = tile.astype(F32)
    return wide[0:1] + wide[1:2] + wide[2:3]


def cumulate(ld_ref, cum_ref, col_ref):
    heads, length = ld_ref.shape
    upper = (iota((length, length), 0) <= iota((length, length), 1)).astype(BF16)
    lower = (iota((length, length), 0) >= iota((length, length), 1)).astype(BF16)
    parts = split3(ld_ref[...])
    cum_ref[...] = mm(parts[0], upper) + mm(parts[1], upper) + mm(parts[2], upper)
    col_ref[...] = mm_nt(lower, parts[0]) + mm_nt(lower, parts[1]) + mm_nt(lower, parts[2])


def update_kernel(k_ref, v_ref, ld_ref, send_ref, cum_ref, col_ref):
    cumulate(ld_ref, cum_ref, col_ref)
    length = k_ref.shape[0]
    for h in range(ld_ref.shape[0]):
        col = col_ref[:, h : h + 1]
        total = col[length - 1 : length]
        scaled = (head(k_ref, h).astype(F32) * jnp.exp(total - col)).astype(BF16)
        update = mm_tn(scaled, head(v_ref, h)).astype(BF16)
        scalars = scalar_rows(jnp.broadcast_to(total, (1, HD)))
        for half in range(2):
            send_ref[2 * h + half, :PIECE] = update[half * PIECE : (half + 1) * PIECE]
            send_ref[2 * h + half, PIECE:] = scalars


def group_kernel(got_ref, send_ref, tot_ref):
    acc = jnp.zeros((PIECE, HD), F32)
    group_total = jnp.zeros((1, HD), F32)
    for m in range(SIDE):
        total = read_scalar_row(got_ref[m, PIECE:])
        tot_ref[m : m + 1] = total
        acc = jnp.exp(total) * acc + got_ref[m, :PIECE].astype(F32)
        group_total = group_total + total
    scalars = scalar_rows(group_total)
    acc = acc.astype(BF16)
    for g in range(SIDE):
        send_ref[g, :PIECE] = acc
        send_ref[g, PIECE:] = scalars


def spread_kernel(me_ref, got_ref, far_ref, tot_ref, send_ref, far_tot_ref):
    group = me_ref[0]
    state = jnp.zeros((PIECE, HD), F32)
    for g in range(SIDE):
        total = read_scalar_row(far_ref[g, PIECE:])
        far_tot_ref[g : g + 1] = total
        state = jnp.where(g < group, jnp.exp(total) * state + far_ref[g, :PIECE].astype(F32), state)
    for m in range(SIDE):
        send_ref[m] = state.astype(BF16)
        state = jnp.exp(tot_ref[m : m + 1]) * state + got_ref[m, :PIECE].astype(F32)


def back_group_kernel(got_ref, tot_ref, send_ref):
    acc = jnp.zeros((PIECE, HD), F32)
    gain = jnp.zeros((1, HD), F32)
    for m in reversed(range(SIDE)):
        acc = jnp.exp(tot_ref[m : m + 1]) * acc + got_ref[m, :PIECE].astype(F32)
        gain = gain + got_ref[m, PIECE:].astype(F32)[0:1]
    feature = iota((HD, HD), 0)
    lane = iota((HD, HD), 1)
    pick = ((feature % 8) == lane).astype(BF16)
    mine = ((iota((SIDE, HD), 1) % 64) // 8) == iota((SIDE, HD), 0)
    picked = sum(mm(jnp.where(mine, part.astype(F32), 0.0).astype(BF16), pick) for part in split3(gain))
    high, mid, low = (part.astype(F32) for part in split3(picked))
    rows = iota((16, HD), 0)
    acc = acc.astype(BF16)
    for g in range(SIDE):
        send_ref[g, :PIECE] = acc
        tile = jnp.where(
            rows == 0, high[g : g + 1], jnp.where(rows == 1, mid[g : g + 1], jnp.where(rows == 2, low[g : g + 1], 0.0))
        )
        send_ref[g, PIECE:] = tile.astype(BF16)


def back_spread_kernel(me_ref, got_ref, far_ref, tot_ref, far_tot_ref, send_ref, gain_ref):
    group = me_ref[0]
    state = jnp.zeros((PIECE, HD), F32)
    gain = jnp.zeros((1, HD), F32)
    for g in reversed(range(SIDE)):
        gain = gain + read_scalar_row(far_ref[g, PIECE:])
        state = jnp.where(
            g > group, jnp.exp(far_tot_ref[g : g + 1]) * state + far_ref[g, :PIECE].astype(F32), state
        )
    gain_ref[...] = gain
    for m in reversed(range(SIDE)):
        send_ref[m] = state.astype(BF16)
        state = jnp.exp(tot_ref[m : m + 1]) * state + got_ref[m, :PIECE].astype(F32)


def within_rows(col, row, i):
    wide = (i + 1) * TILE
    spread = jnp.exp(col[i * TILE : wide] - row[:, :wide])
    causal = iota((TILE, wide), 1) <= i * TILE + iota((TILE, wide), 0)
    return spread, causal


def attention_kernel(q_ref, k_ref, v_ref, og_ref, gain_ref, cum_ref, col_ref, state_ref, att_ref, sums_ref):
    length = q_ref.shape[0]
    squares = [jnp.zeros((TILE, HD), F32) for _ in range(length // TILE)]
    dots = [jnp.zeros((TILE, HD), F32) for _ in range(length // TILE)]
    for h in range(cum_ref.shape[0]):
        q, k, v = head(q_ref, h), head(k_ref, h), head(v_ref, h)
        col, row = col_ref[:, h : h + 1], cum_ref[h : h + 1]
        gain = gain_ref[:, h * HD : (h + 1) * HD]
        carried = jnp.exp(col) * mm(q, state_ref[h * HD : (h + 1) * HD])
        for i in range(length // TILE):
            here, wide = slice(i * TILE, (i + 1) * TILE), (i + 1) * TILE
            spread, causal = within_rows(col, row, i)
            mix = jnp.where(causal, spread * mm_nt(q[here], k[:wide]), 0.0).astype(BF16)
            att = mm(mix, v[:wide]) + carried[here]
            att_ref[here, h * HD : (h + 1) * HD] = att
            upstream = gain * og_ref[here, h * HD : (h + 1) * HD].astype(F32)
            squares[i] = squares[i] + att * att
            dots[i] = dots[i] + att * upstream
    lane = iota((TILE, HD), 1)
    packed = jnp.zeros((TILE, HD), F32)
    count = length // TILE
    for i in range(count):
        packed = jnp.where(lane == i, jnp.sum(squares[i], axis=1, keepdims=True), packed)
        packed = jnp.where(lane == count + i, jnp.sum(dots[i], axis=1, keepdims=True), packed)
    sums = jnp.transpose(packed)[:SIDE]
    for t in range(sums_ref.shape[0]):
        sums_ref[t] = sums


def gradient_kernel(sums_ref, att_ref, og_ref, gain_ref, q_ref, col_ref, grad_ref, send_ref):
    length, features = att_ref.shape
    count = length // TILE
    sums = sums_ref[0]
    for t in range(1, sums_ref.shape[0]):
        sums = sums + sums_ref[t]
    sums = sums / (HEAD_GROUP * HD)
    inverse = lax.rsqrt(sums[:count] + 1e-05)
    slope = inverse * inverse * inverse * sums[count:]
    columns = jnp.transpose(
        jnp.concatenate([inverse, slope, jnp.zeros((TILE - 2 * count, TILE), F32)], axis=0)
    )
    inverse = jnp.concatenate([columns[:, i : i + 1] for i in range(count)], axis=0)
    slope = jnp.concatenate([columns[:, count + i : count + i + 1] for i in range(count)], axis=0)
    gains = []
    for h in range(features // HD):
        att = head(att_ref, h)
        out_grad = head(og_ref, h).astype(F32)
        upstream = gain_ref[:, h * HD : (h + 1) * HD] * out_grad
        grad = (inverse * upstream - slope * att).astype(BF16)
        grad_ref[:, h * HD : (h + 1) * HD] = grad
        gains.append(jnp.sum(out_grad * att * inverse, axis=0, keepdims=True))
        scaled = (head(q_ref, h).astype(F32) * jnp.exp(col_ref[:, h : h + 1])).astype(BF16)
        update = mm_tn(scaled, grad).astype(BF16)
        for half in range(2):
            send_ref[2 * h + half, :PIECE] = update[half * PIECE : (half + 1) * PIECE]
    gain_part = jnp.concatenate(gains, axis=1)
    high, mid, low = (part.astype(F32) for part in split3(gain_part))
    mine = ((iota((SIDE, features), 1) // 8) % 8) == iota((SIDE, features), 0)
    feature, lane = iota((features, HD), 0), iota((features, HD), 1)
    place = (feature // 64) * 8 + feature % 8
    to_high = (place == lane).astype(BF16)
    to_low = (place + 64 == lane).astype(BF16)
    picked = mm(jnp.where(mine, high, 0.0).astype(BF16), to_high) + mm(
        jnp.where(mine, mid, 0.0).astype(BF16), to_low
    )
    rows = iota((16, HD), 0)
    for m in range(SIDE):
        send_ref[m, PIECE:] = jnp.where(rows == 0, picked[m : m + 1], 0.0).astype(BF16)


def final_kernel(
    q_ref, k_ref, v_ref, grad_ref, cum_ref, col_ref, state_ref, back_ref, qg_ref, kg_ref, vg_ref, kacc_ref, vacc_ref
):
    length = q_ref.shape[0]
    for h in range(cum_ref.shape[0]):
        lanes = slice(h * HD, (h + 1) * HD)
        q, k, v, grad = head(q_ref, h), head(k_ref, h), head(v_ref, h), head(grad_ref, h)
        state, back = state_ref[lanes], back_ref[lanes]
        col, row = col_ref[:, h : h + 1], cum_ref[h : h + 1]
        rest = jnp.exp(col[length - 1 : length] - col)
        kacc_ref[...] = rest * mm_nt(v, back)
        vacc_ref[...] = rest * mm(k, back)
        carried = jnp.exp(col) * mm_nt(grad, state)
        for i in range(length // TILE):
            here, wide = slice(i * TILE, (i + 1) * TILE), (i + 1) * TILE
            spread, causal = within_rows(col, row, i)
            spread = jnp.where(causal, spread, 0.0)
            mix = (spread * mm_nt(q[here], k[:wide])).astype(BF16)
            grad_mix = (spread * mm_nt(grad[here], v[:wide])).astype(BF16)
            qg_ref[here, lanes] = (mm(grad_mix, k[:wide]) + carried[here]).astype(BF16)
            kacc_ref[:wide] += mm_tn(grad_mix, q[here])
            vacc_ref[:wide] += mm_tn(mix, grad[here])
        kg_ref[:, lanes] = kacc_ref[...].astype(BF16)
        vg_ref[:, lanes] = vacc_ref[...].astype(BF16)


def call(kernel, outs, *args, scratch=(), smem=0, vmem=24, flops=0):
    specs = [pl.BlockSpec(memory_space=pltpu.SMEM)] * smem
    specs += [pl.BlockSpec(memory_space=pltpu.VMEM)] * (len(args) - smem)
    out_specs = [pl.BlockSpec(memory_space=pltpu.VMEM)] * len(outs)
    return pl.pallas_call(
        kernel,
        out_shape=[jax.ShapeDtypeStruct(shape, dtype) for shape, dtype in outs],
        in_specs=specs,
        out_specs=out_specs,
        scratch_shapes=list(scratch),
        compiler_params=pltpu.CompilerParams(vmem_limit_bytes=vmem * 1024 * 1024),
    )(*args)


def exchange(parts, groups):
    return lax.all_to_all(parts, "seq", 0, 0, tiled=True, axis_index_groups=groups)


def shards(queries, keys, values, out_grad, gain, log_decay):
    length, features = queries.shape
    heads = features // HD
    gain_row = gain.reshape(1, features)
    group = (lax.axis_index("seq") // SIDE).astype(jnp.int32).reshape(1)
    message = ((SIDE, MESSAGE, HD), BF16)
    piece = ((SIDE, PIECE, HD), BF16)
    scalars = ((SIDE, HD), F32)
    send, cum, col = call(
        update_kernel,
        [message, ((heads, length), F32), ((length, heads), F32)],
        keys, values, log_decay.T,
    )
    near = exchange(send, NEAR)
    send, totals = call(group_kernel, [message, scalars], near)
    far = exchange(send, FAR)
    send, far_totals = call(spread_kernel, [piece, scalars], group, near, far, totals, smem=1)
    state = exchange(send, NEAR).reshape(features, HD)
    attention, sums = call(
        attention_kernel,
        [((length, features), F32), ((8, SIDE, HD), F32)],
        queries, keys, values, out_grad, gain_row, cum, col, state,
    )
    sums = lax.all_to_all(sums, "tp", 0, 0, tiled=True)
    grad, send = call(
        gradient_kernel,
        [((length, features), BF16), message],
        sums, attention, out_grad, gain_row, queries, col,
    )
    near = exchange(send, NEAR)
    (send,) = call(back_group_kernel, [message], near, totals)
    far = exchange(send, FAR)
    send, gain_grad = call(
        back_spread_kernel, [piece, ((1, HD), F32)], group, near, far, totals, far_totals, smem=1
    )
    back = exchange(send, NEAR).reshape(features, HD)
    flat = ((length, features), BF16)
    query_grad, key_grad, value_grad = call(
        final_kernel,
        [flat, flat, flat],
        queries, keys, values, grad, cum, col, state, back,
        scratch=[pltpu.VMEM((length, HD), F32)] * 2,
    )
    return query_grad, key_grad, value_grad, gain_grad[0, : features // (SIDE * SIDE)]


def solution(mesh):
    in_specs = (
        P("seq", "tp"),
        P("seq", "tp"),
        P("seq", "tp"),
        P("seq", "tp"),
        P("tp"),
        P("seq", "tp"),
    )
    out_specs = (P("seq", "tp"), P("seq", "tp"), P("seq", "tp"), P(("tp", "seq")))
    return jax.shard_map(shards, mesh=mesh, in_specs=in_specs, out_specs=out_specs, check_vma=False)
```

```python
import jax
import jax.numpy as jnp
from jax import lax
from jax.experimental import pallas as pl
from jax.experimental.pallas import tpu as pltpu
from jax.sharding import PartitionSpec as P

HEAD_GROUP = 32
HD = 128
SIDE = 8
PIECE = 64
MESSAGE = PIECE + 8
TILE = 128
BLOCK = 256
HEAVY = 60 * 1024 * 1024
BF16, F32 = jnp.bfloat16, jnp.float32

NEAR = [[g * SIDE + m for m in range(SIDE)] for g in range(SIDE)]
FAR = [[g * SIDE + m for g in range(SIDE)] for m in range(SIDE)]


def mm(a, b):
    return lax.dot_general(a, b, (((1,), (0,)), ((), ())), preferred_element_type=F32)


def mm_nt(a, b):
    return lax.dot_general(a, b, (((1,), (1,)), ((), ())), preferred_element_type=F32)


def mm_tn(a, b):
    return lax.dot_general(a, b, (((0,), (0,)), ((), ())), preferred_element_type=F32)


def split3(x):
    high = x.astype(BF16)
    rest = x - high.astype(F32)
    mid = rest.astype(BF16)
    low = (rest - mid.astype(F32)).astype(BF16)
    return high, mid, low


def head(ref, h):
    return ref[:, h * HD : (h + 1) * HD]


def iota(shape, dim):
    return lax.broadcasted_iota(jnp.int32, shape, dim)


def rows_of(*parts):
    rows = iota((MESSAGE - PIECE, HD), 0)
    out = jnp.zeros((MESSAGE - PIECE, HD), F32)
    for n, part in enumerate(parts):
        out = jnp.where(rows == n, part.astype(F32), out)
    return out.astype(BF16)


def read_scalar_row(tile):
    wide = tile.astype(F32)
    return wide[0:1] + wide[1:2] + wide[2:3]


def stacked(ref):
    heads, length = ref.shape
    parts = [part.astype(F32) for part in split3(ref[...])]
    return jnp.concatenate(parts + [jnp.zeros((16 - 3 * heads, length), F32)], axis=0).astype(BF16)


def cumulative_columns(ld_ref):
    heads, length = ld_ref.shape
    lower = (iota((length, length), 0) >= iota((length, length), 1)).astype(BF16)
    sums = mm_nt(lower, stacked(ld_ref))
    return sums[:, :heads] + sums[:, heads : 2 * heads] + sums[:, 2 * heads : 3 * heads]


def cumulative_rows(ld_ref):
    heads, length = ld_ref.shape
    upper = (iota((length, length), 0) <= iota((length, length), 1)).astype(BF16)
    sums = mm(stacked(ld_ref), upper)
    return sums[:heads] + sums[heads : 2 * heads] + sums[2 * heads : 3 * heads]


def update_kernel(me_ref, k_hbm, v_hbm, ld_hbm, send_ref, place_ref, k_ref, v_ref, ld_ref, col_ref, sems, ld_sem):
    heads, length = ld_ref.shape
    ld_copy = pltpu.make_async_copy(ld_hbm, ld_ref, ld_sem)
    ld_copy.start()
    place_ref[...] = iota((SIDE, HD), 0) - me_ref[0]
    copies = []
    for n, (hbm, ref) in enumerate(((k_hbm, k_ref), (v_hbm, v_ref))):
        for i in range(length // TILE):
            rows = pl.ds(i * TILE, TILE)
            copies.append(pltpu.make_async_copy(hbm.at[rows], ref.at[rows], sems.at[n, i]))
            copies[-1].start()
    ld_copy.wait()
    col_ref[...] = cumulative_columns(ld_ref)
    for copy in copies:
        copy.wait()
    for h in range(heads):
        col = col_ref[:, h : h + 1]
        total = col[length - 1 : length]
        scaled = (head(k_ref, h).astype(F32) * jnp.exp(total - col)).astype(BF16)
        update = mm_tn(scaled, head(v_ref, h)).astype(BF16)
        scalars = rows_of(*split3(jnp.broadcast_to(total, (1, HD))))
        for half in range(2):
            send_ref[2 * h + half, :PIECE] = update[half * PIECE : (half + 1) * PIECE]
            send_ref[2 * h + half, PIECE:] = scalars


def group_kernel(got_ref, send_ref, tot_ref):
    acc = jnp.zeros((PIECE, HD), F32)
    group_total = jnp.zeros((1, HD), F32)
    for m in range(SIDE):
        total = read_scalar_row(got_ref[m, PIECE:])
        tot_ref[m : m + 1] = total
        acc = jnp.exp(total) * acc + got_ref[m, :PIECE].astype(F32)
        group_total = group_total + total
    scalars = rows_of(*split3(group_total))
    acc = acc.astype(BF16)
    for g in range(SIDE):
        send_ref[g, :PIECE] = acc
        send_ref[g, PIECE:] = scalars


def spread_kernel(got_ref, far_ref, tot_ref, place_ref, send_ref, far_tot_ref):
    state = jnp.zeros((PIECE, HD), F32)
    for g in range(SIDE):
        total = read_scalar_row(far_ref[g, PIECE:])
        far_tot_ref[g : g + 1] = total
        earlier = place_ref[g : g + 1] < 0
        state = jnp.where(earlier, jnp.exp(total) * state + far_ref[g, :PIECE].astype(F32), state)
    for m in range(SIDE):
        send_ref[m] = state.astype(BF16)
        state = jnp.exp(tot_ref[m : m + 1]) * state + got_ref[m, :PIECE].astype(F32)


def back_group_kernel(got_ref, tot_ref, send_ref):
    acc = jnp.zeros((PIECE, HD), F32)
    gain = jnp.zeros((1, HD), F32)
    for m in reversed(range(SIDE)):
        acc = jnp.exp(tot_ref[m : m + 1]) * acc + got_ref[m, :PIECE].astype(F32)
        gain = gain + got_ref[m, PIECE:].astype(F32)[0:1]
    feature = iota((HD, HD), 0)
    lane = iota((HD, HD), 1)
    pick = ((feature % 8) == lane).astype(BF16)
    mine = ((iota((SIDE, HD), 1) % 64) // 8) == iota((SIDE, HD), 0)
    picked = sum(mm(jnp.where(mine, part.astype(F32), 0.0).astype(BF16), pick) for part in split3(gain))
    parts = split3(picked)
    acc = acc.astype(BF16)
    for g in range(SIDE):
        send_ref[g, :PIECE] = acc
        send_ref[g, PIECE:] = rows_of(*(part[g : g + 1] for part in parts))


def back_spread_kernel(got_ref, far_ref, tot_ref, far_tot_ref, place_ref, send_ref, gain_ref):
    state = jnp.zeros((PIECE, HD), F32)
    gain = jnp.zeros((1, HD), F32)
    for g in reversed(range(SIDE)):
        gain = gain + read_scalar_row(far_ref[g, PIECE:])
        later = place_ref[g : g + 1] > 0
        state = jnp.where(later, jnp.exp(far_tot_ref[g : g + 1]) * state + far_ref[g, :PIECE].astype(F32), state)
    gain_ref[...] = gain
    for m in reversed(range(SIDE)):
        send_ref[m] = state.astype(BF16)
        state = jnp.exp(tot_ref[m : m + 1]) * state + got_ref[m, :PIECE].astype(F32)


def causal_tile():
    return iota((BLOCK, BLOCK), 1) <= iota((BLOCK, BLOCK), 0)


def decayed(scores, col, row, i, causal):
    here, start = slice(i * BLOCK, (i + 1) * BLOCK), i * BLOCK
    on = jnp.where(causal, jnp.exp(jnp.where(causal, col[here] - row[:, here], 0.0)), 0.0)
    if i == 0:
        return [(on * score).astype(BF16) for score in scores]
    base = row[:, start - 1 : start]
    off = jnp.exp(col[here] - base) * jnp.exp(base - row[:, :start])
    return [
        jnp.concatenate([(off * score[:, :start]).astype(BF16), (on * score[:, start:]).astype(BF16)], axis=1)
        for score in scores
    ]


def attention_kernel(
    q_ref, k_ref, v_ref, og_ref, gain_ref, ld_ref, state_ref, att_ref, sums_ref, mix_ref, row_ref, col_ref
):
    heads, length = ld_ref.shape
    count = length // TILE
    row_ref[...], col_ref[...] = cumulative_rows(ld_ref), cumulative_columns(ld_ref)
    grow = jnp.exp(col_ref[...])
    causal = causal_tile()
    squares = [jnp.zeros((BLOCK, HD), F32)] * (length // BLOCK)
    dots = [jnp.zeros((BLOCK, HD), F32)] * (length // BLOCK)
    for h in range(heads):
        lanes = slice(h * HD, (h + 1) * HD)
        q, k, v = head(q_ref, h), head(k_ref, h), head(v_ref, h)
        col, row = col_ref[:, h : h + 1], row_ref[h : h + 1]
        carried = grow[:, h : h + 1] * mm(q, state_ref[lanes])
        for i in range(length // BLOCK):
            here, wide = slice(i * BLOCK, (i + 1) * BLOCK), (i + 1) * BLOCK
            (mix,) = decayed([mm_nt(q[here], k[:wide])], col, row, i, causal)
            mix_ref[h, here, :wide] = mix
            att = mm(mix, v[:wide]) + carried[here]
            att_ref[here, lanes] = att
            squares[i] = squares[i] + att * att
            dots[i] = dots[i] + att * (gain_ref[:, lanes] * og_ref[here, lanes].astype(F32))
    squares, dots = jnp.concatenate(squares, axis=0), jnp.concatenate(dots, axis=0)
    lane = iota((TILE, HD), 1)
    packed = jnp.zeros((TILE, HD), F32)
    for i in range(count):
        here = slice(i * TILE, (i + 1) * TILE)
        packed = jnp.where(lane == i, jnp.sum(squares[here], axis=1, keepdims=True), packed)
        packed = jnp.where(lane == count + i, jnp.sum(dots[here], axis=1, keepdims=True), packed)
    sums = jnp.transpose(packed)[:SIDE]
    for t in range(sums_ref.shape[0]):
        sums_ref[t] = sums


def gradient_kernel(sums_ref, att_ref, og_ref, gain_ref, q_ref, col_ref, grad_ref, send_ref):
    length, features = att_ref.shape
    count = length // TILE
    sums = sums_ref[0]
    for t in range(1, sums_ref.shape[0]):
        sums = sums + sums_ref[t]
    sums = sums / (HEAD_GROUP * HD)
    inverse = lax.rsqrt(sums[:count] + 1e-05)
    slope = inverse * inverse * inverse * sums[count:]
    columns = jnp.transpose(
        jnp.concatenate([inverse, slope, jnp.zeros((TILE - 2 * count, TILE), F32)], axis=0)
    )
    inverse = jnp.concatenate([columns[:, i : i + 1] for i in range(count)], axis=0)
    slope = jnp.concatenate([columns[:, count + i : count + i + 1] for i in range(count)], axis=0)
    gains = []
    for h in range(features // HD):
        att = head(att_ref, h)
        out_grad = head(og_ref, h).astype(F32)
        upstream = gain_ref[:, h * HD : (h + 1) * HD] * out_grad
        grad = (inverse * upstream - slope * att).astype(BF16)
        grad_ref[:, h * HD : (h + 1) * HD] = grad
        gains.append(jnp.sum(out_grad * att * inverse, axis=0, keepdims=True))
        scaled = (head(q_ref, h).astype(F32) * jnp.exp(col_ref[:, h : h + 1])).astype(BF16)
        update = mm_tn(scaled, grad).astype(BF16)
        for half in range(2):
            send_ref[2 * h + half, :PIECE] = update[half * PIECE : (half + 1) * PIECE]
    gain_part = jnp.concatenate(gains, axis=1)
    high, mid, low = (part.astype(F32) for part in split3(gain_part))
    mine = ((iota((SIDE, features), 1) // 8) % 8) == iota((SIDE, features), 0)
    feature, lane = iota((features, HD), 0), iota((features, HD), 1)
    place = (feature // 64) * 8 + feature % 8
    to_high = (place == lane).astype(BF16)
    to_low = (place + 64 == lane).astype(BF16)
    picked = mm(jnp.where(mine, high, 0.0).astype(BF16), to_high) + mm(
        jnp.where(mine, mid, 0.0).astype(BF16), to_low
    )
    for m in range(SIDE):
        send_ref[m, PIECE:] = rows_of(picked[m : m + 1])


def final_kernel(
    q_ref, k_ref, v_ref, grad_ref, mix_ref, row_ref, col_ref, state_ref, back_ref, gain_row_ref,
    qg_hbm, kg_hbm, vg_hbm, gain_hbm,
    qg_ref, kg_ref, vg_ref, gain_ref, gmix_ref, sems, gain_sem,
):
    heads, length = row_ref.shape
    gain_ref[...] = gain_row_ref[0, : gain_ref.shape[0]]
    copies = [pltpu.make_async_copy(gain_ref, gain_hbm, gain_sem)]
    copies[0].start()
    causal = causal_tile()
    for h in range(heads):
        lanes = slice(h * HD, (h + 1) * HD)
        q, k, v, grad = head(q_ref, h), head(k_ref, h), head(v_ref, h), head(grad_ref, h)
        back = back_ref[lanes]
        col, row = col_ref[:, h : h + 1], row_ref[h : h + 1]
        rest = jnp.exp(col[length - 1 : length] - col)
        carried = jnp.exp(col) * mm_nt(grad, state_ref[lanes])
        for i in range(length // BLOCK):
            here, wide = slice(i * BLOCK, (i + 1) * BLOCK), (i + 1) * BLOCK
            (gmix,) = decayed([mm_nt(grad[here], v[:wide])], col, row, i, causal)
            gmix_ref[here, :wide] = gmix
            qg_ref[here, lanes] = (mm(gmix, k[:wide]) + carried[here]).astype(BF16)
        key_carried, value_carried = rest * mm_nt(v, back), rest * mm(k, back)
        for j in range(length // BLOCK):
            here, tail = slice(j * BLOCK, (j + 1) * BLOCK), slice(j * BLOCK, length)
            kg_ref[here, lanes] = (mm_tn(gmix_ref[tail, here], q[tail]) + key_carried[here]).astype(BF16)
            vg_ref[here, lanes] = (mm_tn(mix_ref[h, tail, here], grad[tail]) + value_carried[here]).astype(BF16)
        for n, (ref, hbm) in enumerate(((qg_ref, qg_hbm), (kg_ref, kg_hbm), (vg_ref, vg_hbm))):
            lanes = pl.ds(h * HD, HD)
            copies.append(pltpu.make_async_copy(ref.at[:, lanes], hbm.at[:, lanes], sems.at[n, h]))
            copies[-1].start()
    for copy in copies:
        copy.wait()


VMEM, SMEM, HBM = (pl.BlockSpec(memory_space=space) for space in (pltpu.VMEM, pltpu.SMEM, pltpu.HBM))


def call(kernel, outs, *args, ins=None, out_specs=None, scratch=(), vmem=16 * 1024 * 1024):
    return pl.pallas_call(
        kernel,
        out_shape=[jax.ShapeDtypeStruct(shape, dtype) for shape, dtype in outs],
        in_specs=ins or [VMEM] * len(args),
        out_specs=out_specs or [VMEM] * len(outs),
        scratch_shapes=list(scratch),
        compiler_params=pltpu.CompilerParams(vmem_limit_bytes=vmem),
    )(*args)


def exchange(parts, groups):
    return lax.all_to_all(parts, "seq", 0, 0, tiled=True, axis_index_groups=groups)


def shards(queries, keys, values, out_grad, gain, log_decay):
    length, features = queries.shape
    heads = features // HD
    gain_row = gain.reshape(1, features)
    decay_rows = log_decay.T
    group = (lax.axis_index("seq") // SIDE).astype(jnp.int32).reshape(1)
    message = ((SIDE, MESSAGE, HD), BF16)
    piece = ((SIDE, PIECE, HD), BF16)
    scalars = ((SIDE, HD), F32)
    half, whole, columns = ((length, features), BF16), ((length, features), F32), ((length, heads), F32)
    tiles = length // TILE
    place = ((SIDE, HD), jnp.int32)
    staging, dma = pltpu.VMEM(*half), pltpu.SemaphoreType.DMA
    send, place = call(
        update_kernel,
        [message, place],
        group, keys, values, decay_rows,
        ins=[SMEM, HBM, HBM, HBM],
        scratch=[staging, staging, pltpu.VMEM((heads, length), F32), pltpu.VMEM(*columns), dma((2, tiles)), dma],
        vmem=HEAVY,
    )
    near = exchange(send, NEAR)
    send, totals = call(group_kernel, [message, scalars], near)
    far = exchange(send, FAR)
    send, far_totals = call(spread_kernel, [piece, scalars], near, far, totals, place)
    state = exchange(send, NEAR).reshape(features, HD)
    cum_rows, mixes = ((heads, length), F32), ((heads, length, length), BF16)
    attention, sums, mix, row, col = call(
        attention_kernel,
        [whole, ((8, SIDE, HD), F32), mixes, cum_rows, columns],
        queries, keys, values, out_grad, gain_row, decay_rows, state,
    )
    sums = lax.all_to_all(sums, "tp", 0, 0, tiled=True)
    grad, send = call(
        gradient_kernel,
        [half, message],
        sums, attention, out_grad, gain_row, queries, col,
    )
    near = exchange(send, NEAR)
    (send,) = call(back_group_kernel, [message], near, totals)
    far = exchange(send, FAR)
    send, gain_grad = call(back_spread_kernel, [piece, ((1, HD), F32)], near, far, totals, far_totals, place)
    back = exchange(send, NEAR).reshape(features, HD)
    gain_out = ((features // (SIDE * SIDE),), F32)
    return call(
        final_kernel,
        [half, half, half, gain_out],
        queries, keys, values, grad, mix, row, col, state, back, gain_grad,
        out_specs=[HBM] * 4,
        scratch=[staging] * 3 + [pltpu.VMEM(*gain_out), pltpu.VMEM((length, length), BF16), dma((3, heads)), dma],
    )


def solution(mesh):
    in_specs = (
        P("seq", "tp"),
        P("seq", "tp"),
        P("seq", "tp"),
        P("seq", "tp"),
        P("tp"),
        P("seq", "tp"),
    )
    out_specs = (P("seq", "tp"), P("seq", "tp"), P("seq", "tp"), P(("tp", "seq")))
    return jax.shard_map(shards, mesh=mesh, in_specs=in_specs, out_specs=out_specs, check_vma=False)
```

```python
import jax
import jax.numpy as jnp
from jax import lax
from jax.experimental import pallas as pl
from jax.experimental.pallas import tpu as pltpu
from jax.sharding import PartitionSpec as P

HEAD_GROUP = 32
HD = 128
SIDE = 8
PIECE = 64
MESSAGE = PIECE + 8
TILE = 128
BLOCK = 256
BF16, F32 = jnp.bfloat16, jnp.float32

NEAR = [[g * SIDE + m for m in range(SIDE)] for g in range(SIDE)]
FAR = [[g * SIDE + m for g in range(SIDE)] for m in range(SIDE)]


def mm(a, b):
    return lax.dot_general(a, b, (((1,), (0,)), ((), ())), preferred_element_type=F32)


def mm_nt(a, b):
    return lax.dot_general(a, b, (((1,), (1,)), ((), ())), preferred_element_type=F32)


def mm_tn(a, b):
    return lax.dot_general(a, b, (((0,), (0,)), ((), ())), preferred_element_type=F32)


def split3(x):
    high = x.astype(BF16)
    rest = x - high.astype(F32)
    mid = rest.astype(BF16)
    low = (rest - mid.astype(F32)).astype(BF16)
    return high, mid, low


def head(ref, h):
    return ref[:, h * HD : (h + 1) * HD]


def iota(shape, dim):
    return lax.broadcasted_iota(jnp.int32, shape, dim)


def rows_of(*parts):
    rows = iota((MESSAGE - PIECE, HD), 0)
    out = jnp.zeros((MESSAGE - PIECE, HD), F32)
    for n, part in enumerate(parts):
        out = jnp.where(rows == n, part.astype(F32), out)
    return out.astype(BF16)


def read_scalar_row(tile):
    wide = tile.astype(F32)
    return wide[0:1] + wide[1:2] + wide[2:3]


def stacked(ref):
    heads, length = ref.shape
    parts = [part.astype(F32) for part in split3(ref[...])]
    return jnp.concatenate(parts + [jnp.zeros((16 - 3 * heads, length), F32)], axis=0).astype(BF16)


def cumulative(ld_ref):
    heads, length = ld_ref.shape
    upper = (iota((length, length), 0) <= iota((length, length), 1)).astype(BF16)
    sums = mm(stacked(ld_ref), upper)
    rows = sums[:heads] + sums[heads : 2 * heads] + sums[2 * heads : 3 * heads]
    return rows, jnp.transpose(jnp.concatenate([rows, jnp.zeros((8 - heads, length), F32)], axis=0))


def two_heads(ref, pair):
    return ref[:, 2 * pair * HD : 2 * (pair + 1) * HD]


def diagonal(ref, pair):
    first, second = (ref[(2 * pair + n) * HD : (2 * pair + n + 1) * HD] for n in range(2))
    zero = jnp.zeros_like(first)
    return jnp.concatenate(
        [jnp.concatenate([first, zero], axis=1), jnp.concatenate([zero, second], axis=1)], axis=0
    )


def update_kernel(me_ref, k_hbm, v_hbm, ld_hbm, send_ref, k_ref, v_ref, ld_ref, sems, ld_sem):
    heads, length = ld_ref.shape
    ld_copy = pltpu.make_async_copy(ld_hbm, ld_ref, ld_sem)
    ld_copy.start()
    copies = []
    for i in range(length // TILE):
        rows = pl.ds(i * TILE, TILE)
        for n, (hbm, ref) in enumerate(((k_hbm, k_ref), (v_hbm, v_ref))):
            copies.append(pltpu.make_async_copy(hbm.at[rows], ref.at[rows], sems.at[n, i]))
            copies[-1].start()
    ld_copy.wait()
    unused, cols = cumulative(ld_ref)
    total = cols[length - 1 : length]
    rest = jnp.exp(total - cols)
    for copy in copies:
        copy.wait()
    for h in range(heads):
        scaled = (head(k_ref, h).astype(F32) * rest[:, h : h + 1]).astype(BF16)
        update = mm_tn(scaled, head(v_ref, h)).astype(BF16)
        scalars = rows_of(*split3(jnp.broadcast_to(total[:, h : h + 1], (1, HD))))
        for half in range(2):
            send_ref[2 * h + half, :PIECE] = update[half * PIECE : (half + 1) * PIECE]
            send_ref[2 * h + half, PIECE:] = scalars


def group_kernel(got_ref, send_ref, tot_ref):
    acc = jnp.zeros((PIECE, HD), F32)
    group_total = jnp.zeros((1, HD), F32)
    for m in range(SIDE):
        total = read_scalar_row(got_ref[m, PIECE:])
        tot_ref[m : m + 1] = total
        acc = jnp.exp(total) * acc + got_ref[m, :PIECE].astype(F32)
        group_total = group_total + total
    scalars = rows_of(*split3(group_total))
    acc = acc.astype(BF16)
    for g in range(SIDE):
        send_ref[g, :PIECE] = acc
        send_ref[g, PIECE:] = scalars


def spread_kernel(me_ref, got_ref, far_ref, tot_ref, send_ref, far_tot_ref):
    group = me_ref[0]
    state = jnp.zeros((PIECE, HD), F32)
    for g in range(SIDE):
        total = read_scalar_row(far_ref[g, PIECE:])
        far_tot_ref[g : g + 1] = total
        state = jnp.where(g < group, jnp.exp(total) * state + far_ref[g, :PIECE].astype(F32), state)
    for m in range(SIDE):
        send_ref[m] = state.astype(BF16)
        state = jnp.exp(tot_ref[m : m + 1]) * state + got_ref[m, :PIECE].astype(F32)


def back_group_kernel(got_ref, tot_ref, send_ref):
    acc = jnp.zeros((PIECE, HD), F32)
    gain = jnp.zeros((1, HD), F32)
    for m in reversed(range(SIDE)):
        acc = jnp.exp(tot_ref[m : m + 1]) * acc + got_ref[m, :PIECE].astype(F32)
        gain = gain + got_ref[m, PIECE:].astype(F32)[0:1]
    feature = iota((HD, HD), 0)
    lane = iota((HD, HD), 1)
    pick = ((feature % 8) == lane).astype(BF16)
    mine = ((iota((SIDE, HD), 1) % 64) // 8) == iota((SIDE, HD), 0)
    picked = sum(mm(jnp.where(mine, part.astype(F32), 0.0).astype(BF16), pick) for part in split3(gain))
    parts = split3(picked)
    acc = acc.astype(BF16)
    for g in range(SIDE):
        send_ref[g, :PIECE] = acc
        send_ref[g, PIECE:] = rows_of(*(part[g : g + 1] for part in parts))


def back_spread_kernel(me_ref, got_ref, far_ref, tot_ref, far_tot_ref, send_ref, gain_ref):
    group = me_ref[0]
    state = jnp.zeros((PIECE, HD), F32)
    gain = jnp.zeros((1, HD), F32)
    for g in reversed(range(SIDE)):
        gain = gain + read_scalar_row(far_ref[g, PIECE:])
        state = jnp.where(g > group, jnp.exp(far_tot_ref[g : g + 1]) * state + far_ref[g, :PIECE].astype(F32), state)
    gain_ref[...] = gain
    for m in reversed(range(SIDE)):
        send_ref[m] = state.astype(BF16)
        state = jnp.exp(tot_ref[m : m + 1]) * state + got_ref[m, :PIECE].astype(F32)


def causal_tile():
    return iota((BLOCK, BLOCK), 1) <= iota((BLOCK, BLOCK), 0)


def decayed(scores, col, row, i, causal):
    here, start = slice(i * BLOCK, (i + 1) * BLOCK), i * BLOCK
    on = jnp.where(causal, jnp.exp(jnp.where(causal, col[here] - row[:, here], 0.0)), 0.0)
    if i == 0:
        return [(on * score).astype(BF16) for score in scores]
    base = row[:, start - 1 : start]
    off = jnp.exp(col[here] - base) * jnp.exp(base - row[:, :start])
    return [
        jnp.concatenate([(off * score[:, :start]).astype(BF16), (on * score[:, start:]).astype(BF16)], axis=1)
        for score in scores
    ]


def attention_kernel(
    q_ref, k_ref, v_ref, og_ref, gain_hbm, ld_ref, state_ref,
    att_ref, sums_ref, mix_ref, row_ref, col_ref,
    gain_ref, sem,
):
    gain_copy = pltpu.make_async_copy(gain_hbm, gain_ref, sem)
    gain_copy.start()
    heads, length = ld_ref.shape
    count = length // TILE
    row_ref[...], col_ref[...] = cumulative(ld_ref)
    grow = jnp.exp(col_ref[...])
    causal = causal_tile()
    carried = [mm(two_heads(q_ref, pair), diagonal(state_ref, pair)) for pair in range(heads // 2)]
    for h in range(heads):
        lanes = slice(h * HD, (h + 1) * HD)
        q, k, v = head(q_ref, h), head(k_ref, h), head(v_ref, h)
        col, row = col_ref[:, h : h + 1], row_ref[h : h + 1]
        own = grow[:, h : h + 1] * carried[h // 2][:, h % 2 * HD : (h % 2 + 1) * HD]
        for i in range(length // BLOCK):
            here, wide = slice(i * BLOCK, (i + 1) * BLOCK), (i + 1) * BLOCK
            (mix,) = decayed([mm_nt(q[here], k[:wide])], col, row, i, causal)
            mix_ref[h, here, :wide] = mix
            att_ref[here, lanes] = mm(mix, v[:wide]) + own[here]
    gain_copy.wait()
    squares, dots = jnp.zeros((length, HD), F32), jnp.zeros((length, HD), F32)
    for h in range(heads):
        lanes = slice(h * HD, (h + 1) * HD)
        att = att_ref[:, lanes]
        squares = squares + att * att
        dots = dots + att * (gain_ref[:, lanes] * og_ref[:, lanes].astype(F32))
    lane = iota((TILE, HD), 1)
    packed = jnp.zeros((TILE, HD), F32)
    for i in range(count):
        here = slice(i * TILE, (i + 1) * TILE)
        packed = jnp.where(lane == i, jnp.sum(squares[here], axis=1, keepdims=True), packed)
        packed = jnp.where(lane == count + i, jnp.sum(dots[here], axis=1, keepdims=True), packed)
    sums = jnp.transpose(packed)[:SIDE]
    for t in range(sums_ref.shape[0]):
        sums_ref[t] = sums


def gradient_kernel(sums_ref, att_ref, og_ref, gain_ref, q_ref, col_ref, grad_ref, send_ref):
    length, features = att_ref.shape
    count = length // TILE
    sums = sums_ref[0]
    for t in range(1, sums_ref.shape[0]):
        sums = sums + sums_ref[t]
    sums = sums / (HEAD_GROUP * HD)
    inverse = lax.rsqrt(sums[:count] + 1e-05)
    slope = inverse * inverse * inverse * sums[count:]
    columns = jnp.transpose(
        jnp.concatenate([inverse, slope, jnp.zeros((TILE - 2 * count, TILE), F32)], axis=0)
    )
    inverse = jnp.concatenate([columns[:, i : i + 1] for i in range(count)], axis=0)
    slope = jnp.concatenate([columns[:, count + i : count + i + 1] for i in range(count)], axis=0)
    gains = []
    for h in range(features // HD):
        att = head(att_ref, h)
        out_grad = head(og_ref, h).astype(F32)
        upstream = gain_ref[:, h * HD : (h + 1) * HD] * out_grad
        grad = (inverse * upstream - slope * att).astype(BF16)
        grad_ref[:, h * HD : (h + 1) * HD] = grad
        gains.append(jnp.sum(out_grad * att * inverse, axis=0, keepdims=True))
        scaled = (head(q_ref, h).astype(F32) * jnp.exp(col_ref[:, h : h + 1])).astype(BF16)
        update = mm_tn(scaled, grad).astype(BF16)
        for half in range(2):
            send_ref[2 * h + half, :PIECE] = update[half * PIECE : (half + 1) * PIECE]
    gain_part = jnp.concatenate(gains, axis=1)
    high, mid, low = (part.astype(F32) for part in split3(gain_part))
    mine = ((iota((SIDE, features), 1) // 8) % 8) == iota((SIDE, features), 0)
    feature, lane = iota((features, HD), 0), iota((features, HD), 1)
    place = (feature // 64) * 8 + feature % 8
    to_high = (place == lane).astype(BF16)
    to_low = (place + 64 == lane).astype(BF16)
    picked = mm(jnp.where(mine, high, 0.0).astype(BF16), to_high) + mm(
        jnp.where(mine, mid, 0.0).astype(BF16), to_low
    )
    for m in range(SIDE):
        send_ref[m, PIECE:] = rows_of(picked[m : m + 1])


def final_kernel(
    q_ref, k_ref, v_ref, grad_ref, mix_ref, row_ref, col_ref, state_ref, back_ref, gain_row_ref,
    qg_hbm, kg_hbm, vg_hbm, gain_hbm,
    qg_ref, kg_ref, vg_ref, gain_ref, gmix_ref, sems, gain_sem,
):
    heads, length = row_ref.shape
    gain_ref[...] = gain_row_ref[0, : gain_ref.shape[0]]
    copies = [pltpu.make_async_copy(gain_ref, gain_hbm, gain_sem)]
    copies[0].start()
    causal = causal_tile()
    grow, rests = jnp.exp(col_ref[...]), jnp.exp(col_ref[length - 1 : length] - col_ref[...])
    for h in range(heads):
        if h % 2 == 0:
            back = diagonal(back_ref, h // 2)
            query_pair = mm_nt(two_heads(grad_ref, h // 2), diagonal(state_ref, h // 2))
            key_pair = mm_nt(two_heads(v_ref, h // 2), back)
            value_pair = mm(two_heads(k_ref, h // 2), back)
        lanes, mine = slice(h * HD, (h + 1) * HD), slice(h % 2 * HD, (h % 2 + 1) * HD)
        q, k, v, grad = head(q_ref, h), head(k_ref, h), head(v_ref, h), head(grad_ref, h)
        col, row = col_ref[:, h : h + 1], row_ref[h : h + 1]
        rest = rests[:, h : h + 1]
        carried = grow[:, h : h + 1] * query_pair[:, mine]
        for i in range(length // BLOCK):
            here, wide = slice(i * BLOCK, (i + 1) * BLOCK), (i + 1) * BLOCK
            (gmix,) = decayed([mm_nt(grad[here], v[:wide])], col, row, i, causal)
            gmix_ref[here, :wide] = gmix
            qg_ref[here, lanes] = (mm(gmix, k[:wide]) + carried[here]).astype(BF16)
        key_carried, value_carried = rest * key_pair[:, mine], rest * value_pair[:, mine]
        for j in range(length // BLOCK):
            here, tail = slice(j * BLOCK, (j + 1) * BLOCK), slice(j * BLOCK, length)
            kg_ref[here, lanes] = (mm_tn(gmix_ref[tail, here], q[tail]) + key_carried[here]).astype(BF16)
            vg_ref[here, lanes] = (mm_tn(mix_ref[h, tail, here], grad[tail]) + value_carried[here]).astype(BF16)
        for n, (ref, hbm) in enumerate(((qg_ref, qg_hbm), (kg_ref, kg_hbm), (vg_ref, vg_hbm))):
            lanes = pl.ds(h * HD, HD)
            copies.append(pltpu.make_async_copy(ref.at[:, lanes], hbm.at[:, lanes], sems.at[n, h]))
            copies[-1].start()
    for copy in copies:
        copy.wait()


VMEM, SMEM, HBM = (pl.BlockSpec(memory_space=space) for space in (pltpu.VMEM, pltpu.SMEM, pltpu.HBM))


def call(kernel, outs, *args, ins=None, out_specs=None, scratch=(), vmem=16 * 1024 * 1024):
    return pl.pallas_call(
        kernel,
        out_shape=[jax.ShapeDtypeStruct(shape, dtype) for shape, dtype in outs],
        in_specs=ins or [VMEM] * len(args),
        out_specs=out_specs or [VMEM] * len(outs),
        scratch_shapes=list(scratch),
        compiler_params=pltpu.CompilerParams(vmem_limit_bytes=vmem),
    )(*args)


def in_hbm(*arrays):
    return [pltpu.with_memory_space_constraint(x, pltpu.HBM) for x in arrays]


def exchange(parts, groups):
    return lax.all_to_all(parts, "seq", 0, 0, tiled=True, axis_index_groups=groups)


def shards(queries, keys, values, out_grad, gain, log_decay):
    length, features = queries.shape
    heads = features // HD
    gain_row = gain.reshape(1, features)
    decay_rows = log_decay.T
    group = (lax.axis_index("seq") // SIDE).astype(jnp.int32).reshape(1)
    message = ((SIDE, MESSAGE, HD), BF16)
    piece = ((SIDE, PIECE, HD), BF16)
    scalars = ((SIDE, HD), F32)
    half, whole, columns = ((length, features), BF16), ((length, features), F32), ((length, 8), F32)
    staging, dma = pltpu.VMEM(*half), pltpu.SemaphoreType.DMA
    (send,) = call(
        update_kernel,
        [message],
        group, *in_hbm(keys, values, decay_rows),
        ins=[SMEM, HBM, HBM, HBM],
        scratch=[staging, staging, pltpu.VMEM((heads, length), F32), dma((2, length // TILE)), dma],
    )
    near = exchange(send, NEAR)
    send, totals = call(group_kernel, [message, scalars], near)
    far = exchange(send, FAR)
    send, far_totals = call(
        spread_kernel, [piece, scalars], group, near, far, totals, ins=[SMEM] + [VMEM] * 3
    )
    state = exchange(send, NEAR).reshape(features, HD)
    cum_rows, mixes = ((heads, length), F32), ((heads, length, length), BF16)
    attention, sums, mix, row, col = call(
        attention_kernel,
        [whole, ((8, SIDE, HD), F32), mixes, cum_rows, columns],
        queries, keys, values, out_grad, gain_row, decay_rows, state,
        ins=[VMEM] * 4 + [HBM] + [VMEM] * 2,
        scratch=[pltpu.VMEM((1, features), F32), dma],
    )
    sums = lax.all_to_all(sums, "tp", 0, 0, tiled=True)
    grad, send = call(
        gradient_kernel,
        [half, message],
        sums, attention, out_grad, gain_row, queries, col,
    )
    near = exchange(send, NEAR)
    (send,) = call(back_group_kernel, [message], near, totals)
    far = exchange(send, FAR)
    send, gain_grad = call(
        back_spread_kernel,
        [piece, ((1, HD), F32)],
        group, near, far, totals, far_totals,
        ins=[SMEM] + [VMEM] * 4,
    )
    back = exchange(send, NEAR).reshape(features, HD)
    gain_out = ((features // (SIDE * SIDE),), F32)
    return call(
        final_kernel,
        [half, half, half, gain_out],
        queries, keys, values, grad, mix, row, col, state, back, gain_grad,
        out_specs=[HBM] * 4,
        scratch=[staging] * 3 + [pltpu.VMEM(*gain_out), pltpu.VMEM((length, length), BF16), dma((3, heads)), dma],
    )


def solution(mesh):
    in_specs = (
        P("seq", "tp"),
        P("seq", "tp"),
        P("seq", "tp"),
        P("seq", "tp"),
        P("tp"),
        P("seq", "tp"),
    )
    out_specs = (P("seq", "tp"), P("seq", "tp"), P("seq", "tp"), P(("tp", "seq")))
    return jax.shard_map(shards, mesh=mesh, in_specs=in_specs, out_specs=out_specs, check_vma=False)
```

```python
import jax
import jax.numpy as jnp
from jax import lax
from jax.experimental import pallas as pl
from jax.experimental.pallas import tpu as pltpu
from jax.sharding import PartitionSpec as P

HEAD_GROUP = 32
HD = 128
SIDE = 8
PIECE = 64
MESSAGE = PIECE + 8
TILE = 128
BLOCK = 256
BF16, F32 = jnp.bfloat16, jnp.float32

NEAR = [[g * SIDE + m for m in range(SIDE)] for g in range(SIDE)]
FAR = [[g * SIDE + m for g in range(SIDE)] for m in range(SIDE)]


def mm(a, b):
    return lax.dot_general(a, b, (((1,), (0,)), ((), ())), preferred_element_type=F32)


def mm_nt(a, b):
    return lax.dot_general(a, b, (((1,), (1,)), ((), ())), preferred_element_type=F32)


def mm_tn(a, b):
    return lax.dot_general(a, b, (((0,), (0,)), ((), ())), preferred_element_type=F32)


def split3(x):
    high = x.astype(BF16)
    rest = x - high.astype(F32)
    mid = rest.astype(BF16)
    low = (rest - mid.astype(F32)).astype(BF16)
    return high, mid, low


def head(ref, h):
    return ref[:, h * HD : (h + 1) * HD]


def iota(shape, dim):
    return lax.broadcasted_iota(jnp.int32, shape, dim)


def rows_of(*parts):
    rows = iota((MESSAGE - PIECE, HD), 0)
    out = jnp.zeros((MESSAGE - PIECE, HD), F32)
    for n, part in enumerate(parts):
        out = jnp.where(rows == n, part.astype(F32), out)
    return out.astype(BF16)


def read_scalar_row(tile):
    wide = tile.astype(F32)
    return wide[0:1] + wide[1:2] + wide[2:3]


def stacked(ref):
    heads, length = ref.shape
    parts = [part.astype(F32) for part in split3(ref[...])]
    return jnp.concatenate(parts + [jnp.zeros((16 - 3 * heads, length), F32)], axis=0).astype(BF16)


def cumulative(ld_ref):
    heads, length = ld_ref.shape
    upper = (iota((length, length), 0) <= iota((length, length), 1)).astype(BF16)
    sums = mm(stacked(ld_ref), upper)
    rows = sums[:heads] + sums[heads : 2 * heads] + sums[2 * heads : 3 * heads]
    return rows, jnp.transpose(jnp.concatenate([rows, jnp.zeros((8 - heads, length), F32)], axis=0))


def two_heads(ref, pair):
    return ref[:, 2 * pair * HD : 2 * (pair + 1) * HD]


def diagonal(ref, pair):
    first, second = (ref[(2 * pair + n) * HD : (2 * pair + n + 1) * HD] for n in range(2))
    zero = jnp.zeros_like(first)
    return jnp.concatenate(
        [jnp.concatenate([first, zero], axis=1), jnp.concatenate([zero, second], axis=1)], axis=0
    )


def update_kernel(me_ref, k_hbm, v_hbm, ld_hbm, send_ref, k_ref, v_ref, ld_ref, sems, ld_sem):
    heads, length = ld_ref.shape
    ld_copy = pltpu.make_async_copy(ld_hbm, ld_ref, ld_sem)
    ld_copy.start()
    copies = []
    for i in range(length // TILE):
        rows = pl.ds(i * TILE, TILE)
        for n, (hbm, ref) in enumerate(((k_hbm, k_ref), (v_hbm, v_ref))):
            copies.append(pltpu.make_async_copy(hbm.at[rows], ref.at[rows], sems.at[n, i]))
            copies[-1].start()
    ld_copy.wait()
    unused, cols = cumulative(ld_ref)
    total = cols[length - 1 : length]
    rest = jnp.exp(total - cols)
    for copy in copies:
        copy.wait()
    for h in range(heads):
        scaled = (head(k_ref, h).astype(F32) * rest[:, h : h + 1]).astype(BF16)
        update = mm_tn(scaled, head(v_ref, h)).astype(BF16)
        scalars = rows_of(*split3(jnp.broadcast_to(total[:, h : h + 1], (1, HD))))
        for half in range(2):
            send_ref[2 * h + half, :PIECE] = update[half * PIECE : (half + 1) * PIECE]
            send_ref[2 * h + half, PIECE:] = scalars


def group_kernel(got_ref, send_ref, tot_ref):
    acc = jnp.zeros((PIECE, HD), F32)
    group_total = jnp.zeros((1, HD), F32)
    for m in range(SIDE):
        total = read_scalar_row(got_ref[m, PIECE:])
        tot_ref[m : m + 1] = total
        acc = jnp.exp(total) * acc + got_ref[m, :PIECE].astype(F32)
        group_total = group_total + total
    scalars = rows_of(*split3(group_total))
    acc = acc.astype(BF16)
    for g in range(SIDE):
        send_ref[g, :PIECE] = acc
        send_ref[g, PIECE:] = scalars


def spread_kernel(me_ref, got_ref, far_ref, tot_ref, send_ref, far_tot_ref):
    group = me_ref[0]
    state = jnp.zeros((PIECE, HD), F32)
    for g in range(SIDE):
        total = read_scalar_row(far_ref[g, PIECE:])
        far_tot_ref[g : g + 1] = total
        state = jnp.where(g < group, jnp.exp(total) * state + far_ref[g, :PIECE].astype(F32), state)
    for m in range(SIDE):
        send_ref[m] = state.astype(BF16)
        state = jnp.exp(tot_ref[m : m + 1]) * state + got_ref[m, :PIECE].astype(F32)


def back_group_kernel(got_ref, tot_ref, send_ref):
    acc = jnp.zeros((PIECE, HD), F32)
    gain = jnp.zeros((1, HD), F32)
    for m in reversed(range(SIDE)):
        acc = jnp.exp(tot_ref[m : m + 1]) * acc + got_ref[m, :PIECE].astype(F32)
        gain = gain + got_ref[m, PIECE:].astype(F32)[0:1]
    feature = iota((HD, HD), 0)
    lane = iota((HD, HD), 1)
    pick = ((feature % 8) == lane).astype(BF16)
    mine = ((iota((SIDE, HD), 1) % 64) // 8) == iota((SIDE, HD), 0)
    picked = sum(mm(jnp.where(mine, part.astype(F32), 0.0).astype(BF16), pick) for part in split3(gain))
    parts = split3(picked)
    acc = acc.astype(BF16)
    for g in range(SIDE):
        send_ref[g, :PIECE] = acc
        send_ref[g, PIECE:] = rows_of(*(part[g : g + 1] for part in parts))


def back_spread_kernel(me_ref, got_ref, far_ref, tot_ref, far_tot_ref, after_ref, send_ref, gain_ref):
    group = me_ref[0]
    state = jnp.zeros((PIECE, HD), F32)
    gain = jnp.zeros((1, HD), F32)
    for g in reversed(range(SIDE)):
        gain = gain + read_scalar_row(far_ref[g, PIECE:])
        state = jnp.where(g > group, jnp.exp(far_tot_ref[g : g + 1]) * state + far_ref[g, :PIECE].astype(F32), state)
    gain_ref[...] = gain
    for m in reversed(range(SIDE)):
        send_ref[m] = state.astype(BF16)
        state = jnp.exp(tot_ref[m : m + 1]) * state + got_ref[m, :PIECE].astype(F32)


def causal_tile():
    return iota((BLOCK, BLOCK), 1) <= iota((BLOCK, BLOCK), 0)


def decayed(scores, col, row, i, causal):
    here, start = slice(i * BLOCK, (i + 1) * BLOCK), i * BLOCK
    on = jnp.where(causal, jnp.exp(jnp.where(causal, col[here] - row[:, here], 0.0)), 0.0)
    if i == 0:
        return [(on * score).astype(BF16) for score in scores]
    base = row[:, start - 1 : start]
    off = jnp.exp(col[here] - base) * jnp.exp(base - row[:, :start])
    return [
        jnp.concatenate([(off * score[:, :start]).astype(BF16), (on * score[:, start:]).astype(BF16)], axis=1)
        for score in scores
    ]


def inner_kernel(
    q_hbm, k_hbm, v_hbm, gain_hbm, ld_ref, after_ref,
    inner_ref, row_ref, col_ref, gain_ref,
    q_ref, k_ref, v_ref, sems, gain_sem,
):
    heads, length = ld_ref.shape
    gain_copy = pltpu.make_async_copy(gain_hbm, gain_ref, gain_sem)
    gain_copy.start()
    copies = []
    for pair in range(heads // 2):
        lanes = pl.ds(2 * pair * HD, 2 * HD)
        for n, (hbm, ref) in enumerate(((q_hbm, q_ref), (k_hbm, k_ref), (v_hbm, v_ref))):
            copies.append(pltpu.make_async_copy(hbm.at[:, lanes], ref.at[:, lanes], sems.at[n, pair]))
            copies[-1].start()
    row_ref[...], col_ref[...] = cumulative(ld_ref)
    causal = causal_tile()
    for h in range(heads):
        if h % 2 == 0:
            for copy in copies[3 * (h // 2) : 3 * (h // 2 + 1)]:
                copy.wait()
        q, k, v = head(q_ref, h), head(k_ref, h), head(v_ref, h)
        col, row = col_ref[:, h : h + 1], row_ref[h : h + 1]
        for i in range(length // BLOCK):
            here, wide = slice(i * BLOCK, (i + 1) * BLOCK), (i + 1) * BLOCK
            (mix,) = decayed([mm_nt(q[here], k[:wide])], col, row, i, causal)
            inner_ref[here, h * HD : (h + 1) * HD] = mm(mix, v[:wide])
    gain_copy.wait()


def attention_kernel(q_ref, og_ref, gain_ref, inner_ref, col_ref, state_ref, att_ref, sums_ref):
    length, features = q_ref.shape
    heads = features // HD
    count = length // TILE
    grow = jnp.exp(col_ref[...])
    squares, dots = jnp.zeros((length, HD), F32), jnp.zeros((length, HD), F32)
    for h in range(heads):
        lanes, mine = slice(h * HD, (h + 1) * HD), slice(h % 2 * HD, (h % 2 + 1) * HD)
        if h % 2 == 0:
            carried = mm(two_heads(q_ref, h // 2), diagonal(state_ref, h // 2))
        att = inner_ref[:, lanes].astype(F32) + grow[:, h : h + 1] * carried[:, mine]
        att_ref[:, lanes] = att
        squares = squares + att * att
        dots = dots + att * (gain_ref[:, lanes] * og_ref[:, lanes].astype(F32))
    lane = iota((TILE, HD), 1)
    packed = jnp.zeros((TILE, HD), F32)
    for i in range(count):
        here = slice(i * TILE, (i + 1) * TILE)
        packed = jnp.where(lane == i, jnp.sum(squares[here], axis=1, keepdims=True), packed)
        packed = jnp.where(lane == count + i, jnp.sum(dots[here], axis=1, keepdims=True), packed)
    sums = jnp.transpose(packed)[:SIDE]
    for t in range(sums_ref.shape[0]):
        sums_ref[t] = sums


def gradient_kernel(sums_ref, att_ref, og_ref, gain_ref, q_ref, col_ref, grad_ref, send_ref):
    length, features = att_ref.shape
    count = length // TILE
    sums = sums_ref[0]
    for t in range(1, sums_ref.shape[0]):
        sums = sums + sums_ref[t]
    sums = sums / (HEAD_GROUP * HD)
    inverse = lax.rsqrt(sums[:count] + 1e-05)
    slope = inverse * inverse * inverse * sums[count:]
    columns = jnp.transpose(
        jnp.concatenate([inverse, slope, jnp.zeros((TILE - 2 * count, TILE), F32)], axis=0)
    )
    inverse = jnp.concatenate([columns[:, i : i + 1] for i in range(count)], axis=0)
    slope = jnp.concatenate([columns[:, count + i : count + i + 1] for i in range(count)], axis=0)
    gains = []
    for h in range(features // HD):
        att = head(att_ref, h)
        out_grad = head(og_ref, h).astype(F32)
        upstream = gain_ref[:, h * HD : (h + 1) * HD] * out_grad
        grad = (inverse * upstream - slope * att).astype(BF16)
        grad_ref[:, h * HD : (h + 1) * HD] = grad
        gains.append(jnp.sum(out_grad * att * inverse, axis=0, keepdims=True))
        scaled = (head(q_ref, h).astype(F32) * jnp.exp(col_ref[:, h : h + 1])).astype(BF16)
        update = mm_tn(scaled, grad).astype(BF16)
        for half in range(2):
            send_ref[2 * h + half, :PIECE] = update[half * PIECE : (half + 1) * PIECE]
    gain_part = jnp.concatenate(gains, axis=1)
    high, mid, low = (part.astype(F32) for part in split3(gain_part))
    mine = ((iota((SIDE, features), 1) // 8) % 8) == iota((SIDE, features), 0)
    feature, lane = iota((features, HD), 0), iota((features, HD), 1)
    place = (feature // 64) * 8 + feature % 8
    to_high = (place == lane).astype(BF16)
    to_low = (place + 64 == lane).astype(BF16)
    picked = mm(jnp.where(mine, high, 0.0).astype(BF16), to_high) + mm(
        jnp.where(mine, mid, 0.0).astype(BF16), to_low
    )
    for m in range(SIDE):
        send_ref[m, PIECE:] = rows_of(picked[m : m + 1])


def local_grad_kernel(
    q_hbm, k_hbm, v_hbm, grad_ref, row_ref, col_ref, state_ref, after_ref,
    qg_hbm, kacc_ref, vacc_ref,
    q_ref, k_ref, v_ref, qg_ref, mix_ref, gmix_ref, sems, out_sems,
):
    heads, length = row_ref.shape
    ins, outs = [], []
    for pair in range(heads // 2):
        lanes = pl.ds(2 * pair * HD, 2 * HD)
        for n, (hbm, ref) in enumerate(((v_hbm, v_ref), (k_hbm, k_ref), (q_hbm, q_ref))):
            ins.append(pltpu.make_async_copy(hbm.at[:, lanes], ref.at[:, lanes], sems.at[n, pair]))
            ins[-1].start()
    causal = causal_tile()
    grow = jnp.exp(col_ref[...])
    for h in range(heads):
        if h % 2 == 0:
            query_pair = mm_nt(two_heads(grad_ref, h // 2), diagonal(state_ref, h // 2))
            for copy in ins[3 * (h // 2) : 3 * (h // 2 + 1)]:
                copy.wait()
        lanes, mine = slice(h * HD, (h + 1) * HD), slice(h % 2 * HD, (h % 2 + 1) * HD)
        q, k, v, grad = head(q_ref, h), head(k_ref, h), head(v_ref, h), head(grad_ref, h)
        col, row = col_ref[:, h : h + 1], row_ref[h : h + 1]
        carried = grow[:, h : h + 1] * query_pair[:, mine]
        for i in range(length // BLOCK):
            here, wide = slice(i * BLOCK, (i + 1) * BLOCK), (i + 1) * BLOCK
            gmix, mix = decayed([mm_nt(grad[here], v[:wide]), mm_nt(q[here], k[:wide])], col, row, i, causal)
            mix_ref[here, :wide] = mix
            gmix_ref[here, :wide] = gmix
            qg_ref[here, lanes] = (mm(gmix, k[:wide]) + carried[here]).astype(BF16)
        for j in range(length // BLOCK):
            here, tail = slice(j * BLOCK, (j + 1) * BLOCK), slice(j * BLOCK, length)
            kacc_ref[here, lanes] = mm_tn(gmix_ref[tail, here], q[tail]).astype(BF16)
            vacc_ref[here, lanes] = mm_tn(mix_ref[tail, here], grad[tail]).astype(BF16)
        lanes = pl.ds(h * HD, HD)
        outs.append(pltpu.make_async_copy(qg_ref.at[:, lanes], qg_hbm.at[:, lanes], out_sems.at[h]))
        outs[-1].start()
    for copy in outs:
        copy.wait()


def final_kernel(
    k_ref, v_ref, col_ref, back_ref, kacc_ref, vacc_ref, gain_row_ref,
    kg_hbm, vg_hbm, gain_hbm,
    kg_ref, vg_ref, gain_ref, sems, gain_sem,
):
    length = col_ref.shape[0]
    gain_ref[...] = gain_row_ref[0, : gain_ref.shape[0]]
    copies = [pltpu.make_async_copy(gain_ref, gain_hbm, gain_sem)]
    copies[0].start()
    rests = jnp.exp(col_ref[length - 1 : length] - col_ref[...])
    for pair in range(kg_ref.shape[1] // (2 * HD)):
        back = diagonal(back_ref, pair)
        key_pair = mm_nt(two_heads(v_ref, pair), back)
        value_pair = mm(two_heads(k_ref, pair), back)
        for n in range(2):
            h = 2 * pair + n
            lanes, mine, rest = slice(h * HD, (h + 1) * HD), slice(n * HD, (n + 1) * HD), rests[:, h : h + 1]
            kg_ref[:, lanes] = (kacc_ref[:, lanes].astype(F32) + rest * key_pair[:, mine]).astype(BF16)
            vg_ref[:, lanes] = (vacc_ref[:, lanes].astype(F32) + rest * value_pair[:, mine]).astype(BF16)
            for m, (ref, hbm) in enumerate(((kg_ref, kg_hbm), (vg_ref, vg_hbm))):
                lanes = pl.ds(h * HD, HD)
                copies.append(pltpu.make_async_copy(ref.at[:, lanes], hbm.at[:, lanes], sems.at[m, h]))
                copies[-1].start()
    for copy in copies:
        copy.wait()


VMEM, SMEM, HBM = (pl.BlockSpec(memory_space=space) for space in (pltpu.VMEM, pltpu.SMEM, pltpu.HBM))


def call(kernel, outs, *args, ins=None, out_specs=None, scratch=(), vmem=16 * 1024 * 1024, flops=0, moved=0):
    return pl.pallas_call(
        kernel,
        out_shape=[jax.ShapeDtypeStruct(shape, dtype) for shape, dtype in outs],
        in_specs=ins or [VMEM] * len(args),
        out_specs=out_specs or [VMEM] * len(outs),
        scratch_shapes=list(scratch),
        compiler_params=pltpu.CompilerParams(vmem_limit_bytes=vmem),
        cost_estimate=pl.CostEstimate(flops=flops, bytes_accessed=moved, transcendentals=0) if flops else None,
    )(*args)


def in_hbm(*arrays):
    return [pltpu.with_memory_space_constraint(x, pltpu.HBM) for x in arrays]


def exchange(parts, groups):
    return lax.all_to_all(parts, "seq", 0, 0, tiled=True, axis_index_groups=groups)


def shards(queries, keys, values, out_grad, gain, log_decay):
    length, features = queries.shape
    heads = features // HD
    gain_row = gain.reshape(1, features)
    decay_rows = log_decay.T
    group = (lax.axis_index("seq") // SIDE).astype(jnp.int32).reshape(1)
    message = ((SIDE, MESSAGE, HD), BF16)
    piece = ((SIDE, PIECE, HD), BF16)
    scalars = ((SIDE, HD), F32)
    half, whole, columns = ((length, features), BF16), ((length, features), F32), ((length, 8), F32)
    staging, dma = pltpu.VMEM(*half), pltpu.SemaphoreType.DMA
    (send,) = call(
        update_kernel,
        [message],
        group, *in_hbm(keys, values, decay_rows),
        ins=[SMEM, HBM, HBM, HBM],
        scratch=[staging, staging, pltpu.VMEM((heads, length), F32), dma((2, length // TILE)), dma],
    )
    near = exchange(send, NEAR)
    send, totals = call(group_kernel, [message, scalars], near)
    far = exchange(send, FAR)
    send, far_totals = call(
        spread_kernel, [piece, scalars], group, near, far, totals, ins=[SMEM] + [VMEM] * 3
    )
    state = exchange(send, NEAR).reshape(features, HD)
    inner, row, col, gain_row = call(
        inner_kernel,
        [whole, ((heads, length), F32), columns, ((1, features), F32)],
        *in_hbm(queries, keys, values, gain_row), decay_rows, *in_hbm(send),
        ins=[HBM] * 4 + [VMEM, HBM],
        scratch=[staging] * 3 + [dma((3, heads // 2)), dma],
        flops=2_000_000_000, moved=3_000_000,
    )
    attention, sums = call(
        attention_kernel,
        [whole, ((8, SIDE, HD), F32)],
        queries, out_grad, gain_row, inner, col, state,
    )
    sums = lax.all_to_all(sums, "tp", 0, 0, tiled=True)
    grad, send = call(
        gradient_kernel,
        [half, message],
        sums, attention, out_grad, gain_row, queries, col,
    )
    near = exchange(send, NEAR)
    (send,) = call(back_group_kernel, [message], near, totals)
    far = exchange(send, FAR)
    query_grad, key_part, value_part = call(
        local_grad_kernel,
        [half, half, half],
        *in_hbm(queries, keys, values), grad, row, col, state, *in_hbm(send),
        ins=[HBM] * 3 + [VMEM] * 4 + [HBM],
        out_specs=[HBM, VMEM, VMEM],
        scratch=[staging] * 4
        + [pltpu.VMEM((length, length), BF16)] * 2
        + [dma((3, heads // 2)), dma((heads,))],
        flops=4_000_000_000, moved=5_000_000,
    )
    send, gain_grad = call(
        back_spread_kernel,
        [piece, ((1, HD), F32)],
        group, near, far, totals, far_totals, *in_hbm(query_grad),
        ins=[SMEM] + [VMEM] * 4 + [HBM],
    )
    back = exchange(send, NEAR).reshape(features, HD)
    gain_out = ((features // (SIDE * SIDE),), F32)
    key_grad, value_grad, gain_grad = call(
        final_kernel,
        [half, half, gain_out],
        keys, values, col, back, key_part, value_part, gain_grad,
        out_specs=[HBM] * 3,
        scratch=[staging] * 2 + [pltpu.VMEM(*gain_out), dma((2, heads)), dma],
    )
    return query_grad, key_grad, value_grad, gain_grad


def solution(mesh):
    in_specs = (
        P("seq", "tp"),
        P("seq", "tp"),
        P("seq", "tp"),
        P("seq", "tp"),
        P("tp"),
        P("seq", "tp"),
    )
    out_specs = (P("seq", "tp"), P("seq", "tp"), P("seq", "tp"), P(("tp", "seq")))
    return jax.shard_map(shards, mesh=mesh, in_specs=in_specs, out_specs=out_specs, check_vma=False)
```

```python
import jax
import jax.numpy as jnp
from jax import lax
from jax.experimental import pallas as pl
from jax.experimental.pallas import tpu as pltpu
from jax.sharding import PartitionSpec as P

HEAD_GROUP = 32
HD = 128
SIDE = 8
PIECE = 64
MESSAGE = PIECE + 8
TILE = 128
BLOCK = 256
BF16, F32 = jnp.bfloat16, jnp.float32

NEAR = [[g * SIDE + m for m in range(SIDE)] for g in range(SIDE)]
FAR = [[g * SIDE + m for g in range(SIDE)] for m in range(SIDE)]


def mm(a, b):
    return lax.dot_general(a, b, (((1,), (0,)), ((), ())), preferred_element_type=F32)


def mm_nt(a, b):
    return lax.dot_general(a, b, (((1,), (1,)), ((), ())), preferred_element_type=F32)


def mm_tn(a, b):
    return lax.dot_general(a, b, (((0,), (0,)), ((), ())), preferred_element_type=F32)


def split3(x):
    high = x.astype(BF16)
    rest = x - high.astype(F32)
    mid = rest.astype(BF16)
    low = (rest - mid.astype(F32)).astype(BF16)
    return high, mid, low


def head(ref, h):
    return ref[:, h * HD : (h + 1) * HD]


def iota(shape, dim):
    return lax.broadcasted_iota(jnp.int32, shape, dim)


def rows_of(*parts):
    rows = iota((MESSAGE - PIECE, HD), 0)
    out = jnp.zeros((MESSAGE - PIECE, HD), F32)
    for n, part in enumerate(parts):
        out = jnp.where(rows == n, part.astype(F32), out)
    return out.astype(BF16)


def two_parts(rows):
    high, mid, unused = split3(rows)
    return jnp.concatenate([high.astype(F32), mid.astype(F32)], axis=0).astype(BF16)


def read_scalar_row(tile):
    wide = tile.astype(F32)
    return wide[0:1] + wide[1:2] + wide[2:3]


def stacked(ref):
    heads, length = ref.shape
    parts = [part.astype(F32) for part in split3(ref[...])]
    return jnp.concatenate(parts + [jnp.zeros((16 - 3 * heads, length), F32)], axis=0).astype(BF16)


def cumulative(ld_ref):
    heads, length = ld_ref.shape
    upper = (iota((length, length), 0) <= iota((length, length), 1)).astype(BF16)
    sums = mm(stacked(ld_ref), upper)
    rows = sums[:heads] + sums[heads : 2 * heads] + sums[2 * heads : 3 * heads]
    return rows, jnp.transpose(jnp.concatenate([rows, jnp.zeros((8 - heads, length), F32)], axis=0))


def two_heads(ref, pair):
    return ref[:, 2 * pair * HD : 2 * (pair + 1) * HD]


def diagonal(ref, pair):
    first, second = (ref[(2 * pair + n) * HD : (2 * pair + n + 1) * HD] for n in range(2))
    zero = jnp.zeros_like(first)
    return jnp.concatenate(
        [jnp.concatenate([first, zero], axis=1), jnp.concatenate([zero, second], axis=1)], axis=0
    )


def update_kernel(me_ref, k_hbm, v_hbm, ld_hbm, send_ref, k_ref, v_ref, ld_ref, sems, ld_sem):
    heads, length = ld_ref.shape
    ld_copy = pltpu.make_async_copy(ld_hbm, ld_ref, ld_sem)
    ld_copy.start()
    copies = []
    for i in range(length // TILE):
        rows = pl.ds(i * TILE, TILE)
        for n, (hbm, ref) in enumerate(((k_hbm, k_ref), (v_hbm, v_ref))):
            copies.append(pltpu.make_async_copy(hbm.at[rows], ref.at[rows], sems.at[n, i]))
            copies[-1].start()
    ld_copy.wait()
    unused, cols = cumulative(ld_ref)
    total = cols[length - 1 : length]
    rest = jnp.exp(total - cols)
    for copy in copies:
        copy.wait()
    for h in range(heads):
        scaled = (head(k_ref, h).astype(F32) * rest[:, h : h + 1]).astype(BF16)
        update = mm_tn(scaled, head(v_ref, h)).astype(BF16)
        scalars = rows_of(*split3(jnp.broadcast_to(total[:, h : h + 1], (1, HD))))
        for half in range(2):
            send_ref[2 * h + half, :PIECE] = update[half * PIECE : (half + 1) * PIECE]
            send_ref[2 * h + half, PIECE:] = scalars


def group_kernel(got_ref, send_ref, tot_ref):
    acc = jnp.zeros((PIECE, HD), F32)
    group_total = jnp.zeros((1, HD), F32)
    for m in range(SIDE):
        total = read_scalar_row(got_ref[m, PIECE:])
        tot_ref[m : m + 1] = total
        acc = jnp.exp(total) * acc + got_ref[m, :PIECE].astype(F32)
        group_total = group_total + total
    scalars = rows_of(*split3(group_total))
    acc = acc.astype(BF16)
    for g in range(SIDE):
        send_ref[g, :PIECE] = acc
        send_ref[g, PIECE:] = scalars


def spread_kernel(me_ref, got_ref, far_ref, tot_ref, send_ref, far_tot_ref):
    group = lax.div(me_ref[0], SIDE)
    state = jnp.zeros((PIECE, HD), F32)
    for g in range(SIDE):
        total = read_scalar_row(far_ref[g, PIECE:])
        far_tot_ref[g : g + 1] = total
        state = jnp.where(g < group, jnp.exp(total) * state + far_ref[g, :PIECE].astype(F32), state)
    for m in range(SIDE):
        send_ref[m] = state.astype(BF16)
        state = jnp.exp(tot_ref[m : m + 1]) * state + got_ref[m, :PIECE].astype(F32)


def back_group_kernel(got_ref, tot_ref, send_ref):
    acc = jnp.zeros((PIECE, HD), F32)
    gain = jnp.zeros((MESSAGE - PIECE, HD), F32)
    for m in reversed(range(SIDE)):
        acc = jnp.exp(tot_ref[m : m + 1]) * acc + got_ref[m, :PIECE].astype(F32)
        gain = gain + got_ref[m, PIECE:].astype(F32)
    half = gain.shape[0] // 2
    tile = two_parts(gain[:half] + gain[half:])
    acc = acc.astype(BF16)
    for g in range(SIDE):
        send_ref[g, :PIECE] = acc
        send_ref[g, PIECE:] = tile


def back_spread_kernel(me_ref, got_ref, far_ref, tot_ref, far_tot_ref, send_ref, gain_ref):
    group = lax.div(me_ref[0], SIDE)
    state = jnp.zeros((PIECE, HD), F32)
    gain = jnp.zeros((MESSAGE - PIECE, HD), F32)
    for g in reversed(range(SIDE)):
        gain = gain + far_ref[g, PIECE:].astype(F32)
        state = jnp.where(g > group, jnp.exp(far_tot_ref[g : g + 1]) * state + far_ref[g, :PIECE].astype(F32), state)
    gain_ref[...] = gain
    for m in reversed(range(SIDE)):
        send_ref[m] = state.astype(BF16)
        state = jnp.exp(tot_ref[m : m + 1]) * state + got_ref[m, :PIECE].astype(F32)


def causal_tile():
    return iota((BLOCK, BLOCK), 1) <= iota((BLOCK, BLOCK), 0)


def decayed(scores, col, row, i, causal):
    here, start = slice(i * BLOCK, (i + 1) * BLOCK), i * BLOCK
    on = jnp.where(causal, jnp.exp(jnp.where(causal, col[here] - row[:, here], 0.0)), 0.0)
    if i == 0:
        return [(on * score).astype(BF16) for score in scores]
    base = row[:, start - 1 : start]
    off = jnp.exp(col[here] - base) * jnp.exp(base - row[:, :start])
    return [
        jnp.concatenate([(off * score[:, :start]).astype(BF16), (on * score[:, start:]).astype(BF16)], axis=1)
        for score in scores
    ]


def inner_kernel(
    q_hbm, k_hbm, v_hbm, gain_hbm, ld_ref, after_ref,
    inner_ref, sq_ref, row_ref, col_ref, gain_ref,
    q_ref, k_ref, v_ref, sems, gain_sem,
):
    heads, length = ld_ref.shape
    gain_copy = pltpu.make_async_copy(gain_hbm, gain_ref, gain_sem)
    gain_copy.start()
    copies = []
    for pair in range(heads // 2):
        lanes = pl.ds(2 * pair * HD, 2 * HD)
        for n, (hbm, ref) in enumerate(((q_hbm, q_ref), (k_hbm, k_ref), (v_hbm, v_ref))):
            copies.append(pltpu.make_async_copy(hbm.at[:, lanes], ref.at[:, lanes], sems.at[n, pair]))
            copies[-1].start()
    row_ref[...], col_ref[...] = cumulative(ld_ref)
    grow = jnp.exp(col_ref[...])
    causal = causal_tile()
    for h in range(heads):
        if h % 2 == 0:
            for copy in copies[3 * (h // 2) : 3 * (h // 2 + 1)]:
                copy.wait()
        q, k, v = head(q_ref, h), head(k_ref, h), head(v_ref, h)
        col, row = col_ref[:, h : h + 1], row_ref[h : h + 1]
        sq_ref[:, h * HD : (h + 1) * HD] = (q.astype(F32) * grow[:, h : h + 1]).astype(BF16)
        for i in range(length // BLOCK):
            here, wide = slice(i * BLOCK, (i + 1) * BLOCK), (i + 1) * BLOCK
            (mix,) = decayed([mm_nt(q[here], k[:wide])], col, row, i, causal)
            inner_ref[here, h * HD : (h + 1) * HD] = mm(mix, v[:wide])
    gain_copy.wait()


def attention_kernel(sq_ref, og_ref, gain_ref, inner_ref, state_ref, att_ref, sums_ref):
    length, features = sq_ref.shape
    heads = features // HD
    count = length // TILE
    squares, dots = jnp.zeros((length, HD), F32), jnp.zeros((length, HD), F32)
    for h in range(heads):
        lanes, mine = slice(h * HD, (h + 1) * HD), slice(h % 2 * HD, (h % 2 + 1) * HD)
        if h % 2 == 0:
            carried = mm(two_heads(sq_ref, h // 2), diagonal(state_ref, h // 2))
        att = inner_ref[:, lanes] + carried[:, mine]
        att_ref[:, lanes] = att
        squares = squares + att * att
        dots = dots + att * (gain_ref[:, lanes] * og_ref[:, lanes].astype(F32))
    lane = iota((TILE, HD), 1)
    packed = jnp.zeros((TILE, HD), F32)
    for i in range(count):
        here = slice(i * TILE, (i + 1) * TILE)
        packed = jnp.where(lane == i, jnp.sum(squares[here], axis=1, keepdims=True), packed)
        packed = jnp.where(lane == count + i, jnp.sum(dots[here], axis=1, keepdims=True), packed)
    sums = jnp.transpose(packed)[:SIDE]
    for t in range(sums_ref.shape[0]):
        sums_ref[t] = sums


def gradient_kernel(sums_ref, att_ref, og_ref, gain_ref, sq_ref, grad_ref, send_ref):
    length, features = att_ref.shape
    count = length // TILE
    sums = sums_ref[0]
    for t in range(1, sums_ref.shape[0]):
        sums = sums + sums_ref[t]
    sums = sums / (HEAD_GROUP * HD)
    inverse = lax.rsqrt(sums[:count] + 1e-05)
    slope = inverse * inverse * inverse * sums[count:]
    columns = jnp.transpose(
        jnp.concatenate([inverse, slope, jnp.zeros((TILE - 2 * count, TILE), F32)], axis=0)
    )
    inverse = jnp.concatenate([columns[:, i : i + 1] for i in range(count)], axis=0)
    slope = jnp.concatenate([columns[:, count + i : count + i + 1] for i in range(count)], axis=0)
    gains = []
    for h in range(features // HD):
        att = head(att_ref, h)
        normed = inverse * head(og_ref, h).astype(F32)
        grad = (normed * gain_ref[:, h * HD : (h + 1) * HD] - slope * att).astype(BF16)
        grad_ref[:, h * HD : (h + 1) * HD] = grad
        gains.append(jnp.sum(normed * att, axis=0, keepdims=True))
        update = mm_tn(head(sq_ref, h), grad).astype(BF16)
        for half in range(2):
            send_ref[2 * h + half, :PIECE] = update[half * PIECE : (half + 1) * PIECE]
    tile = two_parts(jnp.concatenate(gains, axis=0))
    for m in range(SIDE):
        send_ref[m, PIECE:] = tile


def local_grad_kernel(
    q_hbm, k_ref, v_ref, grad_ref, row_ref, col_ref, state_ref, after_ref,
    qg_hbm, kacc_ref, vacc_ref,
    q_ref, qg_ref, mix_ref, gmix_ref, sems, out_sems,
):
    heads, length = row_ref.shape
    ins, outs = [], []
    for pair in range(heads // 2):
        lanes = pl.ds(2 * pair * HD, 2 * HD)
        ins.append(pltpu.make_async_copy(q_hbm.at[:, lanes], q_ref.at[:, lanes], sems.at[pair]))
        ins[-1].start()
    causal = causal_tile()
    grow = jnp.exp(col_ref[...])
    for h in range(heads):
        if h % 2 == 0:
            query_pair = mm_nt(two_heads(grad_ref, h // 2), diagonal(state_ref, h // 2))
            ins[h // 2].wait()
        lanes, mine = slice(h * HD, (h + 1) * HD), slice(h % 2 * HD, (h % 2 + 1) * HD)
        q, k, v, grad = head(q_ref, h), head(k_ref, h), head(v_ref, h), head(grad_ref, h)
        col, row = col_ref[:, h : h + 1], row_ref[h : h + 1]
        carried = grow[:, h : h + 1] * query_pair[:, mine]
        for i in range(length // BLOCK):
            here, wide = slice(i * BLOCK, (i + 1) * BLOCK), (i + 1) * BLOCK
            gmix, mix = decayed([mm_nt(grad[here], v[:wide]), mm_nt(q[here], k[:wide])], col, row, i, causal)
            mix_ref[here, :wide] = mix
            gmix_ref[here, :wide] = gmix
            qg_ref[here, lanes] = (mm(gmix, k[:wide]) + carried[here]).astype(BF16)
        for j in range(length // BLOCK):
            here, tail = slice(j * BLOCK, (j + 1) * BLOCK), slice(j * BLOCK, length)
            kacc_ref[here, lanes] = mm_tn(gmix_ref[tail, here], q[tail]).astype(BF16)
            vacc_ref[here, lanes] = mm_tn(mix_ref[tail, here], grad[tail]).astype(BF16)
        lanes = pl.ds(h * HD, HD)
        outs.append(pltpu.make_async_copy(qg_ref.at[:, lanes], qg_hbm.at[:, lanes], out_sems.at[h]))
        outs[-1].start()
    for copy in outs:
        copy.wait()


def final_kernel(
    me_ref, k_ref, v_ref, col_ref, back_ref, kacc_ref, vacc_ref, gain_rows_ref,
    kg_hbm, vg_hbm, gain_hbm,
    kg_ref, vg_ref, gain_ref, sems, gain_sem,
):
    length = col_ref.shape[0]
    count = gain_ref.shape[0]
    parts, rows = gain_rows_ref[...], gain_rows_ref.shape[0] // 2
    gains = parts[:rows] + parts[rows:]
    start = me_ref[0] * count
    row = jnp.zeros((1, HD), F32)
    for n in range(rows):
        row = jnp.where(n == start // HD, gains[n : n + 1], row)
    row = pltpu.roll(jnp.broadcast_to(row, (8, HD)), lax.rem(HD - lax.rem(start, HD), HD), 1)
    gain_ref[...] = row[0, :count]
    copies = [pltpu.make_async_copy(gain_ref, gain_hbm, gain_sem)]
    copies[0].start()
    rests = jnp.exp(col_ref[length - 1 : length] - col_ref[...])
    for pair in range(kg_ref.shape[1] // (2 * HD)):
        back = diagonal(back_ref, pair)
        key_pair = mm_nt(two_heads(v_ref, pair), back)
        value_pair = mm(two_heads(k_ref, pair), back)
        for n in range(2):
            h = 2 * pair + n
            lanes, mine, rest = slice(h * HD, (h + 1) * HD), slice(n * HD, (n + 1) * HD), rests[:, h : h + 1]
            kg_ref[:, lanes] = (kacc_ref[:, lanes].astype(F32) + rest * key_pair[:, mine]).astype(BF16)
            vg_ref[:, lanes] = (vacc_ref[:, lanes].astype(F32) + rest * value_pair[:, mine]).astype(BF16)
            for m, (ref, hbm) in enumerate(((kg_ref, kg_hbm), (vg_ref, vg_hbm))):
                lanes = pl.ds(h * HD, HD)
                copies.append(pltpu.make_async_copy(ref.at[:, lanes], hbm.at[:, lanes], sems.at[m, h]))
                copies[-1].start()
    for copy in copies:
        copy.wait()


VMEM, SMEM, HBM = (pl.BlockSpec(memory_space=space) for space in (pltpu.VMEM, pltpu.SMEM, pltpu.HBM))


def call(kernel, outs, *args, ins=None, out_specs=None, scratch=(), vmem=16 * 1024 * 1024, flops=0, moved=0):
    return pl.pallas_call(
        kernel,
        out_shape=[jax.ShapeDtypeStruct(shape, dtype) for shape, dtype in outs],
        in_specs=ins or [VMEM] * len(args),
        out_specs=out_specs or [VMEM] * len(outs),
        scratch_shapes=list(scratch),
        compiler_params=pltpu.CompilerParams(vmem_limit_bytes=vmem),
        cost_estimate=pl.CostEstimate(flops=flops, bytes_accessed=moved, transcendentals=0) if flops else None,
    )(*args)


def in_hbm(*arrays):
    return [pltpu.with_memory_space_constraint(x, pltpu.HBM) for x in arrays]


def exchange(parts, groups):
    return lax.all_to_all(parts, "seq", 0, 0, tiled=True, axis_index_groups=groups)


def shards(queries, keys, values, out_grad, gain, log_decay):
    length, features = queries.shape
    heads = features // HD
    gain_row = gain.reshape(1, features)
    decay_rows = log_decay.T
    place = lax.axis_index("seq").astype(jnp.int32).reshape(1)
    message = ((SIDE, MESSAGE, HD), BF16)
    piece = ((SIDE, PIECE, HD), BF16)
    scalars = ((SIDE, HD), F32)
    half, whole, columns = ((length, features), BF16), ((length, features), F32), ((length, 8), F32)
    staging, dma = pltpu.VMEM(*half), pltpu.SemaphoreType.DMA
    (send,) = call(
        update_kernel,
        [message],
        place, *in_hbm(keys, values, decay_rows),
        ins=[SMEM, HBM, HBM, HBM],
        scratch=[staging, staging, pltpu.VMEM((heads, length), F32), dma((2, length // TILE)), dma],
    )
    near = exchange(send, NEAR)
    send, totals = call(group_kernel, [message, scalars], near)
    far = exchange(send, FAR)
    send, far_totals = call(
        spread_kernel, [piece, scalars], place, near, far, totals, ins=[SMEM] + [VMEM] * 3
    )
    state = exchange(send, NEAR).reshape(features, HD)
    inner, scaled, row, col, gain_row = call(
        inner_kernel,
        [whole, half, ((heads, length), F32), columns, ((1, features), F32)],
        *in_hbm(queries, keys, values, gain_row), decay_rows, *in_hbm(send),
        ins=[HBM] * 4 + [VMEM, HBM],
        scratch=[staging] * 3 + [dma((3, heads // 2)), dma],
        flops=2_000_000_000, moved=3_000_000,
    )
    attention, sums = call(
        attention_kernel,
        [whole, ((8, SIDE, HD), F32)],
        scaled, out_grad, gain_row, inner, state,
    )
    sums = lax.all_to_all(sums, "tp", 0, 0, tiled=True)
    grad, send = call(
        gradient_kernel,
        [half, message],
        sums, attention, out_grad, gain_row, scaled,
    )
    near = exchange(send, NEAR)
    (send,) = call(back_group_kernel, [message], near, totals)
    far = exchange(send, FAR)
    send, gain_grad = call(
        back_spread_kernel,
        [piece, scalars],
        place, near, far, totals, far_totals,
        ins=[SMEM] + [VMEM] * 4,
    )
    query_grad, key_part, value_part = call(
        local_grad_kernel,
        [half, half, half],
        *in_hbm(queries), keys, values, grad, row, col, state, *in_hbm(send),
        ins=[HBM] + [VMEM] * 6 + [HBM],
        out_specs=[HBM, VMEM, VMEM],
        scratch=[staging] * 2
        + [pltpu.VMEM((length, length), BF16)] * 2
        + [dma((heads // 2,)), dma((heads,))],
        flops=4_000_000_000, moved=5_000_000,
    )
    back = exchange(send, NEAR).reshape(features, HD)
    gain_out = ((features // (SIDE * SIDE),), F32)
    key_grad, value_grad, gain_grad = call(
        final_kernel,
        [half, half, gain_out],
        place, keys, values, col, back, key_part, value_part, gain_grad,
        ins=[SMEM] + [VMEM] * 7,
        out_specs=[HBM] * 3,
        scratch=[staging] * 2 + [pltpu.VMEM(*gain_out), dma((2, heads)), dma],
    )
    return query_grad, key_grad, value_grad, gain_grad


def solution(mesh):
    in_specs = (
        P("seq", "tp"),
        P("seq", "tp"),
        P("seq", "tp"),
        P("seq", "tp"),
        P("tp"),
        P("seq", "tp"),
    )
    out_specs = (P("seq", "tp"), P("seq", "tp"), P("seq", "tp"), P(("tp", "seq")))
    return jax.shard_map(shards, mesh=mesh, in_specs=in_specs, out_specs=out_specs, check_vma=False)
```

```python
import jax
import jax.numpy as jnp
from jax import lax
from jax.experimental import pallas as pl
from jax.experimental.pallas import tpu as pltpu
from jax.sharding import PartitionSpec as P

HEAD_GROUP = 32
HD = 128
SIDE = 8
PIECE = 64
MESSAGE = PIECE + 16
TILE = 128
BLOCK = 256
BF16, F32 = jnp.bfloat16, jnp.float32

NEAR = [[g * SIDE + m for m in range(SIDE)] for g in range(SIDE)]
FAR = [[g * SIDE + m for g in range(SIDE)] for m in range(SIDE)]


def mm(a, b):
    return lax.dot_general(a, b, (((1,), (0,)), ((), ())), preferred_element_type=F32)


def mm_nt(a, b):
    return lax.dot_general(a, b, (((1,), (1,)), ((), ())), preferred_element_type=F32)


def mm_tn(a, b):
    return lax.dot_general(a, b, (((0,), (0,)), ((), ())), preferred_element_type=F32)


def split3(x):
    high = x.astype(BF16)
    rest = x - high.astype(F32)
    mid = rest.astype(BF16)
    low = (rest - mid.astype(F32)).astype(BF16)
    return high, mid, low


def head(ref, h):
    return ref[:, h * HD : (h + 1) * HD]


def iota(shape, dim):
    return lax.broadcasted_iota(jnp.int32, shape, dim)


def rows_of(*parts):
    rows = iota((MESSAGE - PIECE, HD), 0)
    out = jnp.zeros((MESSAGE - PIECE, HD), F32)
    for n, part in enumerate(parts):
        out = jnp.where(rows == n, part.astype(F32), out)
    return out.astype(BF16)


def two_parts(rows):
    high, mid, unused = split3(rows)
    rest = jnp.zeros((MESSAGE - PIECE - 2 * rows.shape[0], HD), F32)
    return jnp.concatenate([high.astype(F32), mid.astype(F32), rest], axis=0).astype(BF16)


def read_scalar_row(tile):
    wide = tile.astype(F32)
    return wide[0:1] + wide[1:2] + wide[2:3]


def stacked(ref):
    heads, length = ref.shape
    parts = [part.astype(F32) for part in split3(ref[...])]
    return jnp.concatenate(parts + [jnp.zeros((16 - 3 * heads, length), F32)], axis=0).astype(BF16)


def cumulative(ld_ref):
    heads, length = ld_ref.shape
    upper = (iota((length, length), 0) <= iota((length, length), 1)).astype(BF16)
    sums = mm(stacked(ld_ref), upper)
    rows = sums[:heads] + sums[heads : 2 * heads] + sums[2 * heads : 3 * heads]
    return rows, jnp.transpose(jnp.concatenate([rows, jnp.zeros((8 - heads, length), F32)], axis=0))


def two_heads(ref, pair):
    return ref[:, 2 * pair * HD : 2 * (pair + 1) * HD]


def diagonal(ref, pair):
    first, second = (ref[(2 * pair + n) * HD : (2 * pair + n + 1) * HD] for n in range(2))
    zero = jnp.zeros_like(first)
    return jnp.concatenate(
        [jnp.concatenate([first, zero], axis=1), jnp.concatenate([zero, second], axis=1)], axis=0
    )


def update_kernel(me_ref, k_hbm, v_hbm, ld_hbm, send_ref, k_ref, v_ref, ld_ref, sems, ld_sem):
    heads, length = ld_ref.shape
    ld_copy = pltpu.make_async_copy(ld_hbm, ld_ref, ld_sem)
    ld_copy.start()
    copies = []
    for i in range(length // TILE):
        rows = pl.ds(i * TILE, TILE)
        for n, (hbm, ref) in enumerate(((k_hbm, k_ref), (v_hbm, v_ref))):
            copies.append(pltpu.make_async_copy(hbm.at[rows], ref.at[rows], sems.at[n, i]))
            copies[-1].start()
    ld_copy.wait()
    unused, cols = cumulative(ld_ref)
    total = cols[length - 1 : length]
    rest = jnp.exp(total - cols)
    for copy in copies:
        copy.wait()
    for h in range(heads):
        scaled = (head(k_ref, h).astype(F32) * rest[:, h : h + 1]).astype(BF16)
        update = mm_tn(scaled, head(v_ref, h)).astype(BF16)
        scalars = rows_of(*split3(jnp.broadcast_to(total[:, h : h + 1], (1, HD))))
        for half in range(2):
            send_ref[2 * h + half, :PIECE] = update[half * PIECE : (half + 1) * PIECE]
            send_ref[2 * h + half, PIECE:] = scalars


def group_kernel(got_ref, send_ref, tot_ref):
    acc = jnp.zeros((PIECE, HD), F32)
    group_total = jnp.zeros((1, HD), F32)
    for m in range(SIDE):
        total = read_scalar_row(got_ref[m, PIECE:])
        tot_ref[m : m + 1] = total
        acc = jnp.exp(total) * acc + got_ref[m, :PIECE].astype(F32)
        group_total = group_total + total
    scalars = rows_of(*split3(group_total))
    acc = acc.astype(BF16)
    for g in range(SIDE):
        send_ref[g, :PIECE] = acc
        send_ref[g, PIECE:] = scalars


def spread_kernel(me_ref, got_ref, far_ref, tot_ref, send_ref, far_tot_ref):
    group = lax.div(me_ref[0], SIDE)
    state = jnp.zeros((PIECE, HD), F32)
    for g in range(SIDE):
        total = read_scalar_row(far_ref[g, PIECE:])
        far_tot_ref[g : g + 1] = total
        state = jnp.where(g < group, jnp.exp(total) * state + far_ref[g, :PIECE].astype(F32), state)
    for m in range(SIDE):
        send_ref[m] = state.astype(BF16)
        state = jnp.exp(tot_ref[m : m + 1]) * state + got_ref[m, :PIECE].astype(F32)


def back_group_kernel(got_ref, tot_ref, send_ref):
    acc = jnp.zeros((PIECE, HD), F32)
    gain = jnp.zeros((MESSAGE - PIECE, HD), F32)
    for m in reversed(range(SIDE)):
        acc = jnp.exp(tot_ref[m : m + 1]) * acc + got_ref[m, :PIECE].astype(F32)
        gain = gain + got_ref[m, PIECE:].astype(F32)
    tile = two_parts(gain[:4] + gain[4:8])
    acc = acc.astype(BF16)
    for g in range(SIDE):
        send_ref[g, :PIECE] = acc
        send_ref[g, PIECE:] = tile


def back_spread_kernel(me_ref, got_ref, far_ref, tot_ref, far_tot_ref, send_ref, gain_ref):
    group = lax.div(me_ref[0], SIDE)
    state = jnp.zeros((PIECE, HD), F32)
    gain = jnp.zeros((MESSAGE - PIECE, HD), F32)
    for g in reversed(range(SIDE)):
        gain = gain + far_ref[g, PIECE:].astype(F32)
        state = jnp.where(g > group, jnp.exp(far_tot_ref[g : g + 1]) * state + far_ref[g, :PIECE].astype(F32), state)
    gain_ref[...] = gain[: gain_ref.shape[0]]
    for m in reversed(range(SIDE)):
        send_ref[m] = state.astype(BF16)
        state = jnp.exp(tot_ref[m : m + 1]) * state + got_ref[m, :PIECE].astype(F32)


def causal_tile():
    return iota((BLOCK, BLOCK), 1) <= iota((BLOCK, BLOCK), 0)


def decayed(scores, col, row, i, causal):
    here, start = slice(i * BLOCK, (i + 1) * BLOCK), i * BLOCK
    on = jnp.where(causal, jnp.exp(jnp.where(causal, col[here] - row[:, here], 0.0)), 0.0)
    if i == 0:
        return [(on * score).astype(BF16) for score in scores]
    base = row[:, start - 1 : start]
    off = jnp.exp(col[here] - base) * jnp.exp(base - row[:, :start])
    return [
        jnp.concatenate([(off * score[:, :start]).astype(BF16), (on * score[:, start:]).astype(BF16)], axis=1)
        for score in scores
    ]


def inner_kernel(
    q_hbm, k_hbm, v_hbm, gain_hbm, ld_ref, after_ref,
    inner_ref, sq_ref, row_ref, col_ref, gain_ref,
    q_ref, k_ref, v_ref, sems, gain_sem,
):
    heads, length = ld_ref.shape
    gain_copy = pltpu.make_async_copy(gain_hbm, gain_ref, gain_sem)
    gain_copy.start()
    copies = []
    for pair in range(heads // 2):
        lanes = pl.ds(2 * pair * HD, 2 * HD)
        for n, (hbm, ref) in enumerate(((q_hbm, q_ref), (k_hbm, k_ref), (v_hbm, v_ref))):
            copies.append(pltpu.make_async_copy(hbm.at[:, lanes], ref.at[:, lanes], sems.at[n, pair]))
            copies[-1].start()
    row_ref[...], col_ref[...] = cumulative(ld_ref)
    grow = jnp.exp(col_ref[...])
    causal = causal_tile()
    for h in range(heads):
        if h % 2 == 0:
            for copy in copies[3 * (h // 2) : 3 * (h // 2 + 1)]:
                copy.wait()
        q, k, v = head(q_ref, h), head(k_ref, h), head(v_ref, h)
        col, row = col_ref[:, h : h + 1], row_ref[h : h + 1]
        sq_ref[:, h * HD : (h + 1) * HD] = (q.astype(F32) * grow[:, h : h + 1]).astype(BF16)
        for i in range(length // BLOCK):
            here, wide = slice(i * BLOCK, (i + 1) * BLOCK), (i + 1) * BLOCK
            (mix,) = decayed([mm_nt(q[here], k[:wide])], col, row, i, causal)
            inner_ref[here, h * HD : (h + 1) * HD] = mm(mix, v[:wide])
    gain_copy.wait()


def attention_kernel(sq_ref, og_ref, gain_ref, inner_ref, state_ref, att_ref, sums_ref):
    length, features = sq_ref.shape
    heads = features // HD
    count = length // TILE
    squares, dots = jnp.zeros((length, HD), F32), jnp.zeros((length, HD), F32)
    for h in range(heads):
        lanes, mine = slice(h * HD, (h + 1) * HD), slice(h % 2 * HD, (h % 2 + 1) * HD)
        if h % 2 == 0:
            carried = mm(two_heads(sq_ref, h // 2), diagonal(state_ref, h // 2))
        att = inner_ref[:, lanes] + carried[:, mine]
        att_ref[:, lanes] = att
        squares = squares + att * att
        dots = dots + att * (gain_ref[:, lanes] * og_ref[:, lanes].astype(F32))
    lane = iota((TILE, HD), 1)
    packed = jnp.zeros((TILE, HD), F32)
    for i in range(count):
        here = slice(i * TILE, (i + 1) * TILE)
        packed = jnp.where(lane == i, jnp.sum(squares[here], axis=1, keepdims=True), packed)
        packed = jnp.where(lane == count + i, jnp.sum(dots[here], axis=1, keepdims=True), packed)
    sums = jnp.transpose(packed)[:SIDE]
    for t in range(sums_ref.shape[0]):
        sums_ref[t] = sums


def gradient_kernel(sums_ref, att_ref, og_ref, gain_ref, sq_ref, grad_ref, send_ref):
    length, features = att_ref.shape
    count = length // TILE
    sums = sums_ref[0]
    for t in range(1, sums_ref.shape[0]):
        sums = sums + sums_ref[t]
    sums = sums / (HEAD_GROUP * HD)
    inverse = lax.rsqrt(sums[:count] + 1e-05)
    slope = inverse * inverse * inverse * sums[count:]
    columns = jnp.transpose(
        jnp.concatenate([inverse, slope, jnp.zeros((TILE - 2 * count, TILE), F32)], axis=0)
    )
    inverse = jnp.concatenate([columns[:, i : i + 1] for i in range(count)], axis=0)
    slope = jnp.concatenate([columns[:, count + i : count + i + 1] for i in range(count)], axis=0)
    gains = []
    for h in range(features // HD):
        att = head(att_ref, h)
        normed = inverse * head(og_ref, h).astype(F32)
        grad = (normed * gain_ref[:, h * HD : (h + 1) * HD] - slope * att).astype(BF16)
        grad_ref[:, h * HD : (h + 1) * HD] = grad
        gains.append(jnp.sum(normed * att, axis=0, keepdims=True))
        update = mm_tn(head(sq_ref, h), grad).astype(BF16)
        for half in range(2):
            send_ref[2 * h + half, :PIECE] = update[half * PIECE : (half + 1) * PIECE]
    tile = two_parts(jnp.concatenate(gains, axis=0))
    for m in range(SIDE):
        send_ref[m, PIECE:] = tile


def local_grad_kernel(
    q_hbm, k_ref, v_ref, grad_ref, row_ref, col_ref, state_ref, after_ref,
    qg_hbm, kacc_ref, vacc_ref,
    q_ref, qg_ref, mix_ref, gmix_ref, sems, out_sems,
):
    heads, length = row_ref.shape
    ins, outs = [], []
    for pair in range(heads // 2):
        lanes = pl.ds(2 * pair * HD, 2 * HD)
        ins.append(pltpu.make_async_copy(q_hbm.at[:, lanes], q_ref.at[:, lanes], sems.at[pair]))
        ins[-1].start()
    causal = causal_tile()
    grow = jnp.exp(col_ref[...])
    for h in range(heads):
        if h % 2 == 0:
            query_pair = mm_nt(two_heads(grad_ref, h // 2), diagonal(state_ref, h // 2))
            ins[h // 2].wait()
        lanes, mine = slice(h * HD, (h + 1) * HD), slice(h % 2 * HD, (h % 2 + 1) * HD)
        q, k, v, grad = head(q_ref, h), head(k_ref, h), head(v_ref, h), head(grad_ref, h)
        col, row = col_ref[:, h : h + 1], row_ref[h : h + 1]
        carried = grow[:, h : h + 1] * query_pair[:, mine]
        for i in range(length // BLOCK):
            here, wide = slice(i * BLOCK, (i + 1) * BLOCK), (i + 1) * BLOCK
            gmix, mix = decayed([mm_nt(grad[here], v[:wide]), mm_nt(q[here], k[:wide])], col, row, i, causal)
            mix_ref[here, :wide] = mix
            gmix_ref[here, :wide] = gmix
            qg_ref[here, lanes] = (mm(gmix, k[:wide]) + carried[here]).astype(BF16)
        for j in range(length // BLOCK):
            here, tail = slice(j * BLOCK, (j + 1) * BLOCK), slice(j * BLOCK, length)
            kacc_ref[here, lanes] = mm_tn(gmix_ref[tail, here], q[tail]).astype(BF16)
            vacc_ref[here, lanes] = mm_tn(mix_ref[tail, here], grad[tail]).astype(BF16)
        lanes = pl.ds(h * HD, HD)
        outs.append(pltpu.make_async_copy(qg_ref.at[:, lanes], qg_hbm.at[:, lanes], out_sems.at[h]))
        outs[-1].start()
    for copy in outs:
        copy.wait()


def final_kernel(
    me_ref, k_ref, v_ref, col_ref, back_ref, kacc_ref, vacc_ref, gain_rows_ref,
    kg_hbm, vg_hbm, gain_hbm,
    kg_ref, vg_ref, gain_ref, sems, gain_sem,
):
    length = col_ref.shape[0]
    count = gain_ref.shape[0]
    parts, rows = gain_rows_ref[...], gain_rows_ref.shape[0] // 2
    gains = parts[:rows] + parts[rows:]
    start = me_ref[0] * count
    row = jnp.zeros((1, HD), F32)
    for n in range(rows):
        row = jnp.where(n == start // HD, gains[n : n + 1], row)
    row = pltpu.roll(jnp.broadcast_to(row, (8, HD)), lax.rem(HD - lax.rem(start, HD), HD), 1)
    gain_ref[...] = row[0, :count]
    copies = [pltpu.make_async_copy(gain_ref, gain_hbm, gain_sem)]
    copies[0].start()
    rests = jnp.exp(col_ref[length - 1 : length] - col_ref[...])
    for pair in range(kg_ref.shape[1] // (2 * HD)):
        back = diagonal(back_ref, pair)
        key_pair = mm_nt(two_heads(v_ref, pair), back)
        value_pair = mm(two_heads(k_ref, pair), back)
        for n in range(2):
            h = 2 * pair + n
            lanes, mine, rest = slice(h * HD, (h + 1) * HD), slice(n * HD, (n + 1) * HD), rests[:, h : h + 1]
            kg_ref[:, lanes] = (kacc_ref[:, lanes].astype(F32) + rest * key_pair[:, mine]).astype(BF16)
            vg_ref[:, lanes] = (vacc_ref[:, lanes].astype(F32) + rest * value_pair[:, mine]).astype(BF16)
            for m, (ref, hbm) in enumerate(((kg_ref, kg_hbm), (vg_ref, vg_hbm))):
                lanes = pl.ds(h * HD, HD)
                copies.append(pltpu.make_async_copy(ref.at[:, lanes], hbm.at[:, lanes], sems.at[m, h]))
                copies[-1].start()
    for copy in copies:
        copy.wait()


VMEM, SMEM, HBM = (pl.BlockSpec(memory_space=space) for space in (pltpu.VMEM, pltpu.SMEM, pltpu.HBM))


def call(kernel, outs, *args, ins=None, out_specs=None, scratch=(), vmem=16 * 1024 * 1024, flops=0, moved=0):
    return pl.pallas_call(
        kernel,
        out_shape=[jax.ShapeDtypeStruct(shape, dtype) for shape, dtype in outs],
        in_specs=ins or [VMEM] * len(args),
        out_specs=out_specs or [VMEM] * len(outs),
        scratch_shapes=list(scratch),
        compiler_params=pltpu.CompilerParams(vmem_limit_bytes=vmem),
        cost_estimate=pl.CostEstimate(flops=flops, bytes_accessed=moved, transcendentals=0) if flops else None,
    )(*args)


def in_hbm(*arrays):
    return [pltpu.with_memory_space_constraint(x, pltpu.HBM) for x in arrays]


def exchange(parts, groups):
    return lax.all_to_all(parts, "seq", 0, 0, tiled=True, axis_index_groups=groups)


def shards(queries, keys, values, out_grad, gain, log_decay):
    length, features = queries.shape
    heads = features // HD
    gain_row = gain.reshape(1, features)
    decay_rows = log_decay.T
    place = lax.axis_index("seq").astype(jnp.int32).reshape(1)
    message = ((SIDE, MESSAGE, HD), BF16)
    piece = ((SIDE, PIECE, HD), BF16)
    scalars = ((SIDE, HD), F32)
    half, whole, columns = ((length, features), BF16), ((length, features), F32), ((length, 8), F32)
    staging, dma = pltpu.VMEM(*half), pltpu.SemaphoreType.DMA
    (send,) = call(
        update_kernel,
        [message],
        place, *in_hbm(keys, values, decay_rows),
        ins=[SMEM, HBM, HBM, HBM],
        scratch=[staging, staging, pltpu.VMEM((heads, length), F32), dma((2, length // TILE)), dma],
    )
    near = exchange(send, NEAR)
    send, totals = call(group_kernel, [message, scalars], near)
    far = exchange(send, FAR)
    send, far_totals = call(
        spread_kernel, [piece, scalars], place, near, far, totals, ins=[SMEM] + [VMEM] * 3
    )
    state = exchange(send, NEAR).reshape(features, HD)
    inner, scaled, row, col, gain_row = call(
        inner_kernel,
        [whole, half, ((heads, length), F32), columns, ((1, features), F32)],
        *in_hbm(queries, keys, values, gain_row), decay_rows, *in_hbm(send),
        ins=[HBM] * 4 + [VMEM, HBM],
        scratch=[staging] * 3 + [dma((3, heads // 2)), dma],
        flops=2_000_000_000, moved=3_000_000,
    )
    attention, sums = call(
        attention_kernel,
        [whole, ((8, SIDE, HD), F32)],
        scaled, out_grad, gain_row, inner, state,
    )
    sums = lax.all_to_all(sums, "tp", 0, 0, tiled=True)
    grad, send = call(
        gradient_kernel,
        [half, message],
        sums, attention, out_grad, gain_row, scaled,
    )
    near = exchange(send, NEAR)
    (send,) = call(back_group_kernel, [message], near, totals)
    far = exchange(send, FAR)
    send, gain_grad = call(
        back_spread_kernel,
        [piece, scalars],
        place, near, far, totals, far_totals,
        ins=[SMEM] + [VMEM] * 4,
    )
    query_grad, key_part, value_part = call(
        local_grad_kernel,
        [half, half, half],
        *in_hbm(queries), keys, values, grad, row, col, state, *in_hbm(send),
        ins=[HBM] + [VMEM] * 6 + [HBM],
        out_specs=[HBM, VMEM, VMEM],
        scratch=[staging] * 2
        + [pltpu.VMEM((length, length), BF16)] * 2
        + [dma((heads // 2,)), dma((heads,))],
        flops=4_000_000_000, moved=5_000_000,
    )
    back = exchange(send, NEAR).reshape(features, HD)
    gain_out = ((features // (SIDE * SIDE),), F32)
    key_grad, value_grad, gain_grad = call(
        final_kernel,
        [half, half, gain_out],
        place, keys, values, col, back, key_part, value_part, gain_grad,
        ins=[SMEM] + [VMEM] * 7,
        out_specs=[HBM] * 3,
        scratch=[staging] * 2 + [pltpu.VMEM(*gain_out), dma((2, heads)), dma],
    )
    return query_grad, key_grad, value_grad, gain_grad


def solution(mesh):
    in_specs = (
        P("seq", "tp"),
        P("seq", "tp"),
        P("seq", "tp"),
        P("seq", "tp"),
        P("tp"),
        P("seq", "tp"),
    )
    out_specs = (P("seq", "tp"), P("seq", "tp"), P("seq", "tp"), P(("tp", "seq")))
    return jax.shard_map(shards, mesh=mesh, in_specs=in_specs, out_specs=out_specs, check_vma=False)
```

```python
import jax
import jax.numpy as jnp
from jax import lax
from jax.experimental import pallas as pl
from jax.experimental.pallas import tpu as pltpu
from jax.sharding import PartitionSpec as P

HEAD_GROUP = 32
HD = 128
SIDE = 8
PIECE = 64
MESSAGE = PIECE + 8
TILE = 128
BLOCK = 256
ROWS = 256
BF16, F32 = jnp.bfloat16, jnp.float32

NEAR = [[g * SIDE + m for m in range(SIDE)] for g in range(SIDE)]
FAR = [[g * SIDE + m for g in range(SIDE)] for m in range(SIDE)]


def mm(a, b):
    return lax.dot_general(a, b, (((1,), (0,)), ((), ())), preferred_element_type=F32)


def mm_nt(a, b):
    return lax.dot_general(a, b, (((1,), (1,)), ((), ())), preferred_element_type=F32)


def mm_tn(a, b):
    return lax.dot_general(a, b, (((0,), (0,)), ((), ())), preferred_element_type=F32)


def split3(x):
    high = x.astype(BF16)
    rest = x - high.astype(F32)
    mid = rest.astype(BF16)
    low = (rest - mid.astype(F32)).astype(BF16)
    return high, mid, low


def head(ref, h):
    return ref[:, h * HD : (h + 1) * HD]


def iota(shape, dim):
    return lax.broadcasted_iota(jnp.int32, shape, dim)


def rows_of(*parts):
    rows = iota((MESSAGE - PIECE, HD), 0)
    out = jnp.zeros((MESSAGE - PIECE, HD), F32)
    for n, part in enumerate(parts):
        out = jnp.where(rows == n, part.astype(F32), out)
    return out.astype(BF16)


def two_parts(rows):
    high, mid, unused = split3(rows)
    return jnp.concatenate([high.astype(F32), mid.astype(F32)], axis=0).astype(BF16)


def read_scalar_row(tile):
    wide = tile.astype(F32)
    return wide[0:1] + wide[1:2] + wide[2:3]


def stacked(ref):
    heads, length = ref.shape
    parts = [part.astype(F32) for part in split3(ref[...])]
    return jnp.concatenate(parts + [jnp.zeros((16 - 3 * heads, length), F32)], axis=0).astype(BF16)


def cumulative(ld_ref):
    heads, length = ld_ref.shape
    upper = (iota((length, length), 0) <= iota((length, length), 1)).astype(BF16)
    sums = mm(stacked(ld_ref), upper)
    rows = sums[:heads] + sums[heads : 2 * heads] + sums[2 * heads : 3 * heads]
    return rows, jnp.transpose(jnp.concatenate([rows, jnp.zeros((8 - heads, length), F32)], axis=0))


def two_heads(ref, pair):
    return ref[:, 2 * pair * HD : 2 * (pair + 1) * HD]


def diagonal(ref, pair):
    first, second = (ref[(2 * pair + n) * HD : (2 * pair + n + 1) * HD] for n in range(2))
    zero = jnp.zeros_like(first)
    return jnp.concatenate(
        [jnp.concatenate([first, zero], axis=1), jnp.concatenate([zero, second], axis=1)], axis=0
    )


def update_kernel(me_ref, k_hbm, v_hbm, ld_hbm, send_ref, k_ref, v_ref, ld_ref, sems, ld_sem):
    heads, length = ld_ref.shape
    ld_copy = pltpu.make_async_copy(ld_hbm, ld_ref, ld_sem)
    ld_copy.start()
    copies = []
    for i in range(length // TILE):
        rows = pl.ds(i * TILE, TILE)
        for n, (hbm, ref) in enumerate(((k_hbm, k_ref), (v_hbm, v_ref))):
            copies.append(pltpu.make_async_copy(hbm.at[rows], ref.at[rows], sems.at[n, i]))
            copies[-1].start()
    ld_copy.wait()
    unused, cols = cumulative(ld_ref)
    total = cols[length - 1 : length]
    rest = jnp.exp(total - cols)
    for copy in copies:
        copy.wait()
    for h in range(heads):
        scaled = (head(v_ref, h).astype(F32) * rest[:, h : h + 1]).astype(BF16)
        update = mm_tn(head(k_ref, h), scaled).astype(BF16)
        scalars = rows_of(*split3(jnp.broadcast_to(total[:, h : h + 1], (1, HD))))
        for half in range(2):
            send_ref[2 * h + half, :PIECE] = update[half * PIECE : (half + 1) * PIECE]
            send_ref[2 * h + half, PIECE:] = scalars


def group_kernel(got_ref, send_ref, tot_ref):
    acc = jnp.zeros((PIECE, HD), F32)
    group_total = jnp.zeros((1, HD), F32)
    for m in range(SIDE):
        total = read_scalar_row(got_ref[m, PIECE:])
        tot_ref[m : m + 1] = total
        acc = jnp.exp(total) * acc + got_ref[m, :PIECE].astype(F32)
        group_total = group_total + total
    scalars = rows_of(*split3(group_total))
    acc = acc.astype(BF16)
    for g in range(SIDE):
        send_ref[g, :PIECE] = acc
        send_ref[g, PIECE:] = scalars


def spread_kernel(me_ref, got_ref, far_ref, tot_ref, send_ref, far_tot_ref):
    group = lax.div(me_ref[0], SIDE)
    state = jnp.zeros((PIECE, HD), F32)
    for g in range(SIDE):
        total = read_scalar_row(far_ref[g, PIECE:])
        far_tot_ref[g : g + 1] = total
        state = jnp.where(g < group, jnp.exp(total) * state + far_ref[g, :PIECE].astype(F32), state)
    for m in range(SIDE):
        send_ref[m] = state.astype(BF16)
        state = jnp.exp(tot_ref[m : m + 1]) * state + got_ref[m, :PIECE].astype(F32)


def back_group_kernel(got_ref, tot_ref, send_ref):
    acc = jnp.zeros((PIECE, HD), F32)
    gain = jnp.zeros((MESSAGE - PIECE, HD), F32)
    for m in reversed(range(SIDE)):
        acc = jnp.exp(tot_ref[m : m + 1]) * acc + got_ref[m, :PIECE].astype(F32)
        gain = gain + got_ref[m, PIECE:].astype(F32)
    half = gain.shape[0] // 2
    tile = two_parts(gain[:half] + gain[half:])
    acc = acc.astype(BF16)
    for g in range(SIDE):
        send_ref[g, :PIECE] = acc
        send_ref[g, PIECE:] = tile


def back_spread_kernel(me_ref, got_ref, far_ref, tot_ref, far_tot_ref, send_ref, gain_ref):
    group = lax.div(me_ref[0], SIDE)
    state = jnp.zeros((PIECE, HD), F32)
    gain = jnp.zeros((MESSAGE - PIECE, HD), F32)
    for g in reversed(range(SIDE)):
        gain = gain + far_ref[g, PIECE:].astype(F32)
        state = jnp.where(g > group, jnp.exp(far_tot_ref[g : g + 1]) * state + far_ref[g, :PIECE].astype(F32), state)
    gain_ref[...] = gain
    for m in reversed(range(SIDE)):
        send_ref[m] = state.astype(BF16)
        state = jnp.exp(tot_ref[m : m + 1]) * state + got_ref[m, :PIECE].astype(F32)


def causal_tile():
    return iota((BLOCK, BLOCK), 1) <= iota((BLOCK, BLOCK), 0)


def decayed(scores, col, row, i, causal):
    here, start = slice(i * BLOCK, (i + 1) * BLOCK), i * BLOCK
    on = jnp.where(causal, jnp.exp(jnp.where(causal, col[here] - row[:, here], 0.0)), 0.0)
    if i == 0:
        return [(on * score).astype(BF16) for score in scores]
    base = row[:, start - 1 : start]
    off = jnp.exp(col[here] - base) * jnp.exp(base - row[:, :start])
    return [
        jnp.concatenate([(off * score[:, :start]).astype(BF16), (on * score[:, start:]).astype(BF16)], axis=1)
        for score in scores
    ]


def inner_kernel(
    q_hbm, k_hbm, v_hbm, gain_hbm, ld_ref, after_ref,
    inner_ref, sq_ref, row_ref, col_ref, gain_ref,
    q_ref, k_ref, v_ref, sems, gain_sem,
):
    heads, length = ld_ref.shape
    gain_copy = pltpu.make_async_copy(gain_hbm, gain_ref, gain_sem)
    gain_copy.start()
    copies = []
    for pair in range(heads // 2):
        lanes = pl.ds(2 * pair * HD, 2 * HD)
        for n, (hbm, ref) in enumerate(((q_hbm, q_ref), (k_hbm, k_ref), (v_hbm, v_ref))):
            copies.append(pltpu.make_async_copy(hbm.at[:, lanes], ref.at[:, lanes], sems.at[n, pair]))
            copies[-1].start()
    row_ref[...], col_ref[...] = cumulative(ld_ref)
    grow = jnp.exp(col_ref[...])
    causal = causal_tile()
    for h in range(heads):
        if h % 2 == 0:
            for copy in copies[3 * (h // 2) : 3 * (h // 2 + 1)]:
                copy.wait()
        q, k, v = head(q_ref, h), head(k_ref, h), head(v_ref, h)
        col, row = col_ref[:, h : h + 1], row_ref[h : h + 1]
        sq_ref[:, h * HD : (h + 1) * HD] = (q.astype(F32) * grow[:, h : h + 1]).astype(BF16)
        for i in range(length // BLOCK):
            here, wide = slice(i * BLOCK, (i + 1) * BLOCK), (i + 1) * BLOCK
            (mix,) = decayed([mm_nt(q[here], k[:wide])], col, row, i, causal)
            inner_ref[here, h * HD : (h + 1) * HD] = mm(mix, v[:wide])
    gain_copy.wait()


def attention_kernel(sq_ref, og_ref, gain_ref, inner_ref, state_ref, att_ref, sums_ref):
    length, features = sq_ref.shape
    heads = features // HD
    count = length // TILE
    squares, dots = jnp.zeros((length, HD), F32), jnp.zeros((length, HD), F32)
    for h in range(heads):
        lanes, mine = slice(h * HD, (h + 1) * HD), slice(h % 2 * HD, (h % 2 + 1) * HD)
        if h % 2 == 0:
            carried = mm(two_heads(sq_ref, h // 2), diagonal(state_ref, h // 2))
        att = inner_ref[:, lanes] + carried[:, mine]
        att_ref[:, lanes] = att
        squares = squares + att * att
        dots = dots + att * (gain_ref[:, lanes] * og_ref[:, lanes].astype(F32))
    lane = iota((TILE, HD), 1)
    packed = jnp.zeros((TILE, HD), F32)
    for i in range(count):
        here = slice(i * TILE, (i + 1) * TILE)
        packed = jnp.where(lane == i, jnp.sum(squares[here], axis=1, keepdims=True), packed)
        packed = jnp.where(lane == count + i, jnp.sum(dots[here], axis=1, keepdims=True), packed)
    sums = jnp.transpose(packed)[:SIDE]
    for t in range(sums_ref.shape[0]):
        sums_ref[t] = sums


def gradient_kernel(sums_ref, att_ref, og_ref, gain_ref, sq_ref, grad_ref, send_ref):
    length, features = att_ref.shape
    count = length // TILE
    sums = sums_ref[0]
    for t in range(1, sums_ref.shape[0]):
        sums = sums + sums_ref[t]
    sums = sums / (HEAD_GROUP * HD)
    inverse = lax.rsqrt(sums[:count] + 1e-05)
    slope = inverse * inverse * inverse * sums[count:]
    columns = jnp.transpose(
        jnp.concatenate([inverse, slope, jnp.zeros((TILE - 2 * count, TILE), F32)], axis=0)
    )
    inverse = jnp.concatenate([columns[:, i : i + 1] for i in range(count)], axis=0)
    slope = jnp.concatenate([columns[:, count + i : count + i + 1] for i in range(count)], axis=0)
    gains = []
    for h in range(features // HD):
        att = head(att_ref, h)
        normed = inverse * head(og_ref, h).astype(F32)
        grad = (normed * gain_ref[:, h * HD : (h + 1) * HD] - slope * att).astype(BF16)
        grad_ref[:, h * HD : (h + 1) * HD] = grad
        gains.append(jnp.sum(normed * att, axis=0, keepdims=True))
        update = mm_tn(head(sq_ref, h), grad).astype(BF16)
        for half in range(2):
            send_ref[2 * h + half, :PIECE] = update[half * PIECE : (half + 1) * PIECE]
    tile = two_parts(jnp.concatenate(gains, axis=0))
    for m in range(SIDE):
        send_ref[m, PIECE:] = tile


def local_grad_kernel(
    q_hbm, k_ref, v_ref, grad_ref, row_ref, col_ref, state_ref, after_ref,
    qg_hbm, kacc_ref, vacc_ref,
    q_ref, qg_ref, mix_ref, gmix_ref, sems, out_sems,
):
    heads, length = row_ref.shape
    ins, outs = [], []
    for pair in range(heads // 2):
        lanes = pl.ds(2 * pair * HD, 2 * HD)
        ins.append(pltpu.make_async_copy(q_hbm.at[:, lanes], q_ref.at[:, lanes], sems.at[pair]))
        ins[-1].start()
    causal = causal_tile()
    grow = jnp.exp(col_ref[...])
    for h in range(heads):
        if h % 2 == 0:
            query_pair = mm_nt(two_heads(grad_ref, h // 2), diagonal(state_ref, h // 2))
            ins[h // 2].wait()
        lanes, mine = slice(h * HD, (h + 1) * HD), slice(h % 2 * HD, (h % 2 + 1) * HD)
        q, k, v, grad = head(q_ref, h), head(k_ref, h), head(v_ref, h), head(grad_ref, h)
        col, row = col_ref[:, h : h + 1], row_ref[h : h + 1]
        carried = grow[:, h : h + 1] * query_pair[:, mine]
        for i in range(length // BLOCK):
            here, wide = slice(i * BLOCK, (i + 1) * BLOCK), (i + 1) * BLOCK
            gmix, mix = decayed([mm_nt(grad[here], v[:wide]), mm_nt(q[here], k[:wide])], col, row, i, causal)
            mix_ref[here, :wide] = mix
            gmix_ref[here, :wide] = gmix
            qg_ref[here, lanes] = (mm(gmix, k[:wide]) + carried[here]).astype(BF16)
        for j in range(length // BLOCK):
            here, tail = slice(j * BLOCK, (j + 1) * BLOCK), slice(j * BLOCK, length)
            kacc_ref[here, lanes] = mm_tn(gmix_ref[tail, here], q[tail]).astype(BF16)
            vacc_ref[here, lanes] = mm_tn(mix_ref[tail, here], grad[tail]).astype(BF16)
        lanes = pl.ds(h * HD, HD)
        outs.append(pltpu.make_async_copy(qg_ref.at[:, lanes], qg_hbm.at[:, lanes], out_sems.at[h]))
        outs[-1].start()
    for copy in outs:
        copy.wait()


def final_kernel(
    me_ref, k_ref, v_ref, col_ref, back_ref, kacc_ref, vacc_ref, gain_rows_ref,
    kg_hbm, vg_hbm, gain_hbm,
    kg_ref, vg_ref, gain_ref, sems, gain_sem,
):
    length = col_ref.shape[0]
    count = gain_ref.shape[0]
    parts, rows = gain_rows_ref[...], gain_rows_ref.shape[0] // 2
    gains = parts[:rows] + parts[rows:]
    start = me_ref[0] * count
    row = jnp.zeros((1, HD), F32)
    for n in range(rows):
        row = jnp.where(n == start // HD, gains[n : n + 1], row)
    row = pltpu.roll(jnp.broadcast_to(row, (8, HD)), lax.rem(HD - lax.rem(start, HD), HD), 1)
    gain_ref[...] = row[0, :count]
    copies = [pltpu.make_async_copy(gain_ref, gain_hbm, gain_sem)]
    copies[0].start()
    rests = jnp.exp(col_ref[length - 1 : length] - col_ref[...])
    backs = [diagonal(back_ref, pair) for pair in range(kg_ref.shape[1] // (2 * HD))]
    for i in range(length // ROWS):
        here = slice(i * ROWS, (i + 1) * ROWS)
        for pair, back in enumerate(backs):
            lanes = slice(2 * pair * HD, 2 * (pair + 1) * HD)
            key_pair, value_pair = mm_nt(v_ref[here, lanes], back), mm(k_ref[here, lanes], back)
            for n in range(2):
                h = 2 * pair + n
                lanes, mine, rest = slice(h * HD, (h + 1) * HD), slice(n * HD, (n + 1) * HD), rests[here, h : h + 1]
                kg_ref[here, lanes] = (kacc_ref[here, lanes].astype(F32) + rest * key_pair[:, mine]).astype(BF16)
                vg_ref[here, lanes] = (vacc_ref[here, lanes].astype(F32) + rest * value_pair[:, mine]).astype(BF16)
        rows = pl.ds(i * ROWS, ROWS)
        for m, (ref, hbm) in enumerate(((kg_ref, kg_hbm), (vg_ref, vg_hbm))):
            copies.append(pltpu.make_async_copy(ref.at[rows], hbm.at[rows], sems.at[m, i]))
            copies[-1].start()
    for copy in copies:
        copy.wait()


VMEM, SMEM, HBM = (pl.BlockSpec(memory_space=space) for space in (pltpu.VMEM, pltpu.SMEM, pltpu.HBM))


def call(kernel, outs, *args, ins=None, out_specs=None, scratch=(), vmem=16 * 1024 * 1024, flops=0, moved=0):
    return pl.pallas_call(
        kernel,
        out_shape=[jax.ShapeDtypeStruct(shape, dtype) for shape, dtype in outs],
        in_specs=ins or [VMEM] * len(args),
        out_specs=out_specs or [VMEM] * len(outs),
        scratch_shapes=list(scratch),
        compiler_params=pltpu.CompilerParams(vmem_limit_bytes=vmem),
        cost_estimate=pl.CostEstimate(flops=flops, bytes_accessed=moved, transcendentals=0) if flops else None,
    )(*args)


def in_hbm(*arrays):
    return [pltpu.with_memory_space_constraint(x, pltpu.HBM) for x in arrays]


def exchange(parts, groups):
    return lax.all_to_all(parts, "seq", 0, 0, tiled=True, axis_index_groups=groups)


def shards(queries, keys, values, out_grad, gain, log_decay):
    length, features = queries.shape
    heads = features // HD
    gain_row = gain.reshape(1, features)
    decay_rows = log_decay.T
    place = lax.axis_index("seq").astype(jnp.int32).reshape(1)
    message = ((SIDE, MESSAGE, HD), BF16)
    piece = ((SIDE, PIECE, HD), BF16)
    scalars = ((SIDE, HD), F32)
    half, whole, columns = ((length, features), BF16), ((length, features), F32), ((length, 8), F32)
    staging, dma = pltpu.VMEM(*half), pltpu.SemaphoreType.DMA
    (send,) = call(
        update_kernel,
        [message],
        place, *in_hbm(keys, values, decay_rows),
        ins=[SMEM, HBM, HBM, HBM],
        scratch=[staging, staging, pltpu.VMEM((heads, length), F32), dma((2, length // TILE)), dma],
    )
    near = exchange(send, NEAR)
    send, totals = call(group_kernel, [message, scalars], near)
    far = exchange(send, FAR)
    send, far_totals = call(
        spread_kernel, [piece, scalars], place, near, far, totals, ins=[SMEM] + [VMEM] * 3
    )
    state = exchange(send, NEAR).reshape(features, HD)
    inner, scaled, row, col, gain_row = call(
        inner_kernel,
        [whole, half, ((heads, length), F32), columns, ((1, features), F32)],
        *in_hbm(queries, keys, values, gain_row), decay_rows, *in_hbm(send),
        ins=[HBM] * 4 + [VMEM, HBM],
        scratch=[staging] * 3 + [dma((3, heads // 2)), dma],
        flops=2_000_000_000, moved=3_000_000,
    )
    attention, sums = call(
        attention_kernel,
        [whole, ((8, SIDE, HD), F32)],
        scaled, out_grad, gain_row, inner, state,
    )
    sums = lax.all_to_all(sums, "tp", 0, 0, tiled=True)
    grad, send = call(
        gradient_kernel,
        [half, message],
        sums, attention, out_grad, gain_row, scaled,
    )
    near = exchange(send, NEAR)
    (send,) = call(back_group_kernel, [message], near, totals)
    far = exchange(send, FAR)
    send, gain_grad = call(
        back_spread_kernel,
        [piece, scalars],
        place, near, far, totals, far_totals,
        ins=[SMEM] + [VMEM] * 4,
    )
    query_grad, key_part, value_part = call(
        local_grad_kernel,
        [half, half, half],
        *in_hbm(queries), keys, values, grad, row, col, state, *in_hbm(send),
        ins=[HBM] + [VMEM] * 6 + [HBM],
        out_specs=[HBM, VMEM, VMEM],
        scratch=[staging] * 2
        + [pltpu.VMEM((length, length), BF16)] * 2
        + [dma((heads // 2,)), dma((heads,))],
        flops=4_000_000_000, moved=5_000_000,
    )
    back = exchange(send, NEAR).reshape(features, HD)
    gain_out = ((features // (SIDE * SIDE),), F32)
    key_grad, value_grad, gain_grad = call(
        final_kernel,
        [half, half, gain_out],
        place, keys, values, col, back, key_part, value_part, gain_grad,
        ins=[SMEM] + [VMEM] * 7,
        out_specs=[HBM] * 3,
        scratch=[staging] * 2 + [pltpu.VMEM(*gain_out), dma((2, length // ROWS)), dma],
    )
    return query_grad, key_grad, value_grad, gain_grad


def solution(mesh):
    in_specs = (
        P("seq", "tp"),
        P("seq", "tp"),
        P("seq", "tp"),
        P("seq", "tp"),
        P("tp"),
        P("seq", "tp"),
    )
    out_specs = (P("seq", "tp"), P("seq", "tp"), P("seq", "tp"), P(("tp", "seq")))
    return jax.shard_map(shards, mesh=mesh, in_specs=in_specs, out_specs=out_specs, check_vma=False)
```
